256 devices in a mesh: grp: 8 (over z), cur: 32 (over y, x, core).
Axes of the slice: x: 4, y: 4, z: 8, core: 2. Of those that a mesh axis runs over, the one named last changes fastest.
Arguments:
- right_side: float32 [3, 2097152], P(None, ('grp', 'cur')), may hold values from -6 to 6
- precond: float32 [2097152], P(('grp', 'cur')), may hold values from 0.3 to 3
- viscosity: float32 [262144], P(('grp', 'cur')), may hold values from 0.1 to 10
- stiffness: float32 [81, 81], replicated
- element_nodes: int32 [27, 262144], P(None, ('grp', 'cur')), may hold values from 0 to 9471
- live_elements: int32 [256], P(('grp', 'cur')), may hold values from 256 to 1024, as said below
- shared_nodes: int32 [2, 131072], P(None, ('grp', 'cur')), may hold values from 0 to 8191, as said below
- hanging_parents: int32 [3, 65536], P(None, ('grp', 'cur')), may hold values from 0 to 9215
Outputs:
- solution: float32 [3, 2097152], P(None, ('grp', 'cur'))
- residual: float32 [3, 2097152], P(None, ('grp', 'cur'))
The draws below stay inside these ranges and needn't reach their ends.
Inputs may be any that keep to these rules, and one draw needn't show every extreme that they name: `element_nodes`: local numbers: below 8192 owned, then 512 copies from the previous device, 512 from the next, then the hanging nodes. `hanging_parents`: parents are owned nodes or copies. `shared_nodes`: within one device, the 1024 entries are distinct owned nodes (no node in both rows). `live_elements`: some device has all 1024 slots live.
All inputs are finite; a program needn't handle non-finite values.
Results may differ from the reference program's by a relative error of at most 0.0004.
Values sent between devices are 32-bit elements; how exact they have to be, the bound alone decides.
A program may use at most 128 MiB of HBM per device.

```python
import math
import jax
import jax.numpy as jnp
from jax import lax

E_DEV = 1024
ITERS = 3
NOD_DEV = 8192
GHOST = 512
HANG = 256
ELEMS = 262144
NODES = 2097152
N_GRP = 8
N_CUR = 32


def draw_stiffness(key, part):
    key = jax.random.fold_in(key, 11)
    key_diag, key_off = jax.random.split(key, 2)
    diagonal = jax.random.uniform(key_diag, (81,), jnp.float32, 0.8, 1.2)
    off_diag = jax.random.uniform(key_off, (81, 81), jnp.float32, -0.0098, 0.0098)
    eye_mask = jnp.eye(81, dtype=jnp.float32)
    return off_diag * (1.0 - eye_mask) + eye_mask * diagonal[None, :]


def draw_live_elements(key, part):
    key = jax.random.fold_in(key, 12)
    key_count, key_full = jax.random.split(key)
    devices = N_GRP * N_CUR
    counts = jax.random.randint(key_count, (devices,), E_DEV // 4, E_DEV + 1)
    fullest = jax.random.randint(key_full, (), 0, devices)
    return counts.at[fullest].set(E_DEV).astype(jnp.int32)


def draw_shared_nodes(key, part):
    key = jax.random.fold_in(key, 13)
    devices = N_GRP * N_CUR
    keys = jax.random.split(key, devices)
    chosen = jax.vmap(lambda one_key: jax.random.permutation(one_key, NOD_DEV)[:2 * GHOST])(keys)
    return chosen.reshape(devices, 2, GHOST).transpose(1, 0, 2).reshape(2, devices * GHOST).astype(jnp.int32)


def plant(result, key, smallest, largest):
    extent = result.shape
    spot = [jax.random.randint(jax.random.fold_in(key, axis), (), 0, extent[axis]) for axis in range(len(extent))]
    result = result.at[tuple(spot)].set(smallest)
    longest = extent.index(max(extent))
    spot[longest] = (spot[longest] + 1) % extent[longest]
    return result.at[tuple(spot)].set(largest)


def block_levels(key, extent, shards, least, largest):
    factor_of, own = 1.0, jax.random.fold_in(key, 6)
    for dim, parts in shards:
        steps = jnp.exp(jax.random.uniform(jax.random.fold_in(own, dim), (parts,), jnp.float32, least / len(shards), largest / len(shards)))
        factor_of = factor_of * jnp.repeat(steps, extent[dim] // parts).reshape([-1 if axis == dim else 1 for axis in range(len(extent))])
    return factor_of


def centred(stream_key, extent, deviation, reach, pieces=(), kind=jnp.bfloat16):
    values = deviation * jax.random.normal(stream_key, extent, jnp.float32)
    if pieces:
        values = values * block_levels(stream_key, extent, pieces, -0.22, 0.18)
    return jnp.clip(values, -reach, reach).astype(kind)


def setup_inputs(seed: int = 0) -> dict:
    seeds = jax.random.split(jax.random.key(seed), 9)
    right_side = centred(seeds[0], (3, NODES), 1.0, 6.0, ((1, 256),), jnp.float32)
    precond = jnp.clip(jnp.exp(math.log(3.0) - 2.3025851 * jax.random.uniform(seeds[1], (NODES,), jnp.float32) ** block_levels(seeds[1], (NODES,), ((0, 256),), -0.2, 0.2)), 0.3, 3.0)
    viscosity = jnp.clip(jnp.exp(math.log(10.0) - 4.6051702 * jax.random.uniform(seeds[2], (ELEMS,), jnp.float32) ** block_levels(seeds[2], (ELEMS,), ((0, 256),), -0.2, 0.2)), 0.1, 10.0)
    stiffness = draw_stiffness(jax.random.fold_in(seeds[8], 71), 0)
    element_nodes = plant(jax.random.randint(seeds[4], (27, ELEMS), 0, NOD_DEV + 2 * GHOST + HANG), jax.random.fold_in(seeds[4], 1), 0, (NOD_DEV + 2 * GHOST + HANG) - 1).astype(jnp.int32)
    live_elements = draw_live_elements(jax.random.fold_in(seeds[8], 71), 0)
    shared_nodes = draw_shared_nodes(jax.random.fold_in(seeds[8], 71), 0)
    hanging_parents = plant(jax.random.randint(seeds[7], (3, HANG * N_GRP * N_CUR), 0, NOD_DEV + 2 * GHOST), jax.random.fold_in(seeds[7], 1), 0, (NOD_DEV + 2 * GHOST) - 1).astype(jnp.int32)
    return {"right_side": right_side, "precond": precond, "viscosity": viscosity, "stiffness": stiffness, "element_nodes": element_nodes, "live_elements": live_elements, "shared_nodes": shared_nodes, "hanging_parents": hanging_parents}


def add_hanging(base, parents):
    hanging = 0.375 * base[:, parents[0]] + 0.75 * base[:, parents[1]] - 0.125 * base[:, parents[2]]
    return jnp.concatenate([base, hanging], 1)


def fold_hanging(partial_value, width, parents):
    hanging_part = partial_value[:, width:]
    base_part = partial_value[:, :width]
    base_part = base_part.at[:, parents[0]].add(0.375 * hanging_part)
    base_part = base_part.at[:, parents[1]].add(0.75 * hanging_part)
    return base_part.at[:, parents[2]].add(-0.125 * hanging_part)


def element_partial(base, parents, cells, visc, live_count, stiffness):
    extended = add_hanging(base, parents)
    width = cells.shape[1]
    flat = cells.reshape(-1)
    values_in = extended[:, flat].reshape(81, width)
    live_mask = (jnp.arange(width) < live_count).astype(jnp.float32)
    weighting = visc * live_mask
    values_out = jnp.dot(stiffness.T, values_in, precision=lax.Precision.HIGHEST) * weighting[None, :]
    partial_value = jnp.zeros((3, extended.shape[1]), jnp.float32).at[:, flat].add(values_out.reshape(3, 27 * width))
    return fold_hanging(partial_value, base.shape[1], parents)


def reference(right_side, precond, viscosity, stiffness, element_nodes, live_elements, shared_nodes, hanging_parents):
    devices = N_GRP * N_CUR

    def split_dev(array):
        return array.reshape(array.shape[0], devices, -1).transpose(1, 0, 2)

    sends = split_dev(shared_nodes)
    parents = split_dev(hanging_parents)
    cells = split_dev(element_nodes)
    visc = viscosity.reshape(devices, E_DEV)
    scaling = precond.reshape(devices, 1, NOD_DEV)
    residual = split_dev(right_side)
    zeros_ghost = jnp.zeros((1, 3, GHOST), jnp.float32)

    def operator(search):
        to_left = jax.vmap(lambda field, index: field[:, index])(search, sends[:, 0])
        to_right = jax.vmap(lambda field, index: field[:, index])(search, sends[:, 1])
        left_ghost = jnp.concatenate([zeros_ghost, to_right[:-1]], 0)
        right_ghost = jnp.concatenate([to_left[1:], zeros_ghost], 0)
        base = jnp.concatenate([search, left_ghost, right_ghost], 2)

        def one_device(items):
            base_one, parent_one, cell_one, visc_one, count_one = items
            return element_partial(base_one, parent_one, cell_one, visc_one, count_one, stiffness)

        partial_value = lax.map(one_device, (base, parents, cells, visc, live_elements))
        owned_part = partial_value[:, :, :NOD_DEV]
        left_part = partial_value[:, :, NOD_DEV:NOD_DEV + GHOST]
        right_part = partial_value[:, :, NOD_DEV + GHOST:]
        from_left = jnp.concatenate([zeros_ghost, right_part[:-1]], 0)
        from_right = jnp.concatenate([left_part[1:], zeros_ghost], 0)
        return jax.vmap(lambda own, index, first, second: own.at[:, index[0]].add(first).at[:, index[1]].add(second))(owned_part, sends, from_left, from_right)

    solution = jnp.zeros_like(residual)
    search = scaling * residual
    norm_now = jnp.sum(residual * search)
    for iteration in range(ITERS):
        image = operator(search)
        step_size = norm_now / jnp.sum(search * image)
        solution = solution + step_size * search
        residual = residual - step_size * image
        search = scaling * residual
        norm_now = jnp.sum(residual * search)
    return solution.transpose(1, 0, 2).reshape(3, -1), residual.transpose(1, 0, 2).reshape(3, -1)
```

```python
import functools

import jax
import jax.numpy as jnp
from jax import lax
from jax.experimental import pallas as pl
from jax.experimental.pallas import tpu as pltpu
from jax.sharding import PartitionSpec as P

ITERS = 3
F32 = jnp.float32
BF16 = jnp.bfloat16
MESH = pl.DeviceIdType.MESH
OWN_ROWS = 64
EXT_ROWS = 74
STEP_K = 3


def take(src, lanes):
    return jnp.take_along_axis(src, lanes, axis=1, mode="promise_in_bounds")


def gather_tile(fields, row_count, index):
    lanes = index & 127
    rows = index >> 7
    found = [jnp.zeros((8, 128), F32) for _ in fields]
    for row in range(row_count):
        hit = rows == row
        for i, field in enumerate(fields):
            line = jnp.broadcast_to(field(row), (8, 128))
            found[i] = jnp.where(hit, take(line, lanes), found[i])
    return found


def folded(index):
    row = index >> 7
    lane = index & 127
    own = row < 64
    hang = row >= 72
    band = jnp.where(own, row & 31, jnp.where(hang, 36, 32 + (row & 3)))
    half = jnp.where(own, row >> 5, jnp.where(hang, row & 1, (row >> 2) & 1))
    return band, half * 128 + lane


def pieces(row):
    high = row.astype(BF16)
    low = (row - high.astype(F32)).astype(BF16)
    return high, low


def spread_dot(band, place, values, extra=True):
    n = band.shape[1]
    band16 = band.astype(jnp.int16)
    place16 = place.astype(jnp.int16)
    zero = jnp.zeros((16, n), BF16)
    one = jnp.ones((256, n), BF16)
    hot = jnp.where(
        lax.broadcasted_iota(jnp.int16, (256, n), 0) == place16, one, jnp.zeros((256, n), BF16)
    )
    line = lax.broadcasted_iota(jnp.int16, (16, n), 0)
    hit0 = line == band16
    hit1 = (line + jnp.int16(16)) == band16
    parts = []
    tails = []
    if extra:
        first = line < jnp.int16(8)
        hit2 = jnp.where(first, line, line - jnp.int16(8)) == (band16 - jnp.int16(32))
    for value in values:
        high, low = pieces(value)
        high = jnp.broadcast_to(high, (16, n))
        low = jnp.broadcast_to(low, (16, n))
        for piece in (high, low):
            parts.append(jnp.where(hit0, piece, zero))
            parts.append(jnp.where(hit1, piece, zero))
        if extra:
            tails.append(jnp.where(hit2, jnp.where(first, high, low), zero))
    left = jnp.concatenate(parts + tails, 0)
    return lax.dot_general(left, hot, (((1,), (1,)), ((), ())), preferred_element_type=F32)


def own_part(total, c):
    return total[c * 64 : c * 64 + 32] + total[c * 64 + 32 : c * 64 + 64]


def extra_part(total, c):
    return total[192 + c * 16 : 200 + c * 16] + total[200 + c * 16 : 208 + c * 16]


def kernel(
    rounds,
    sizes,
    rhs_ref,
    pre_ref,
    visc_ref,
    stiff_ref,
    cells_ref,
    live_ref,
    shared_ref,
    parents_ref,
    sol_ref,
    res_ref,
    ext_ref,
    gres_ref,
    gpre_ref,
    band_ref,
    place_ref,
    u_ref,
    t_ref,
    acc_ref,
    part_ref,
    send_ref,
    recv_ref,
    red_ref,
    sum_ref,
    send_sem,
    recv_sem,
    rsend_sem,
    rrecv_sem,
):
    n_grp, n_cur = sizes
    devices = n_grp * n_cur
    my_grp = lax.axis_index("grp")
    my_cur = lax.axis_index("cur")
    me = my_grp * n_cur + my_cur

    def ring(offset):
        other = lax.rem(me + offset + devices, devices)
        return {"grp": other // n_cur, "cur": lax.rem(other, n_cur)}

    def partner(r, j):
        axis, stride, size = rounds[r]
        mine = my_cur if axis == "cur" else my_grp
        place = lax.rem(mine // stride, size)
        return {axis: mine + (lax.rem(place + j, size) - place) * stride}

    def my_place(r):
        axis, stride, size = rounds[r]
        mine = my_cur if axis == "cur" else my_grp
        return lax.rem(mine // stride, size)

    barrier = pltpu.get_barrier_semaphore()
    targets = [ring(-1), ring(1)]
    for r, (_, _, size) in enumerate(rounds):
        targets += [partner(r, j) for j in range(1, size)]
    for target in targets:
        pl.semaphore_signal(barrier, inc=1, device_id=target, device_id_type=MESH)

    band, place = folded(cells_ref[...])
    band_ref[0:27, :] = band
    place_ref[0:27, :] = place
    shared_index = jnp.concatenate(
        [shared_ref[j : j + 1, q * 128 : (q + 1) * 128] for j in range(2) for q in range(4)], 0
    )
    parent_rows = [parents_ref[p : p + 1, q * 128 : (q + 1) * 128] for p in range(3) for q in range(2)]
    parent_index = jnp.concatenate(parent_rows + parent_rows[:2], 0)
    shared_band, shared_place = folded(
        jnp.concatenate([shared_ref[0:1, :], shared_ref[1:2, :]], 1)
    )
    parent_band, parent_place = folded(
        jnp.concatenate([parents_ref[p : p + 1, :] for p in range(3)], 1)
    )
    slot = lax.broadcasted_iota(jnp.int32, (1, 1024), 1)
    weight = jnp.where(slot < live_ref[0], visc_ref[...], 0.0)
    at = lax.broadcasted_iota(jnp.int32, (96, 81), 0)
    want = jnp.where((at & 31) < 27, (at >> 5) * 27 + (at & 31), -1)
    pick = jnp.where(want == lax.broadcasted_iota(jnp.int32, (96, 81), 1), 1.0, 0.0).astype(BF16)

    def padded(part):
        rows = lax.dot_general(pick, part, (((1,), (1,)), ((), ())), preferred_element_type=F32)
        return lax.dot_general(
            rows.astype(BF16), pick, (((1,), (1,)), ((), ())), preferred_element_type=F32
        ).astype(BF16)

    stiff = stiff_ref[...]
    stiff_high = stiff.astype(BF16)
    stiff_low = padded((stiff - stiff_high.astype(F32)).astype(BF16))
    stiff_high = padded(stiff_high)

    u_ref[...] = jnp.zeros_like(u_ref)
    for c in range(3):
        res_ref[c] = rhs_ref[c]
        sol_ref[c] = jnp.zeros((OWN_ROWS, 128), F32)
        ext_ref[c, 0:OWN_ROWS, :] = pre_ref[...] * rhs_ref[c]

    def exchange(number):
        copies = []
        for side, offset in ((0, -1), (1, 1)):
            copies.append(
                pltpu.make_async_remote_copy(
                    src_ref=send_ref.at[number, side],
                    dst_ref=recv_ref.at[number, 1 - side],
                    send_sem=send_sem.at[number, side],
                    recv_sem=recv_sem.at[number, 1 - side],
                    device_id=ring(offset),
                    device_id_type=MESH,
                )
            )
        for copy in copies:
            copy.start()
        return copies

    outgoing = gather_tile(
        [lambda row, c=c: rhs_ref[c, row : row + 1, :] for c in range(3)]
        + [lambda row: pre_ref[row : row + 1, :]],
        OWN_ROWS,
        shared_index,
    )
    for side in range(2):
        for c in range(3):
            send_ref[0, side, c, 0:4, :] = outgoing[c][side * 4 : side * 4 + 4]
            send_ref[0, side, c, 4:8, :] = outgoing[3][side * 4 : side * 4 + 4]
    pl.semaphore_wait(barrier, len(targets))
    copies = exchange(0)
    for copy in copies:
        copy.wait()
    has = [
        jnp.where(me > 0, 1.0, 0.0).astype(F32),
        jnp.where(me < devices - 1, 1.0, 0.0).astype(F32),
    ]
    for side in range(2):
        for c in range(3):
            gres_ref[c, side * 4 : side * 4 + 4, :] = recv_ref[0, side, c, 0:4, :]
        gpre_ref[side * 4 : side * 4 + 4, :] = recv_ref[0, side, 0, 4:8, :] * has[side]
    for c in range(3):
        ext_ref[c, OWN_ROWS : OWN_ROWS + 8, :] = gpre_ref[...] * gres_ref[c]

    def reduce_send(it, r):
        _, _, size = rounds[r]
        spot = my_place(r)
        sends = []
        for j in range(1, size):
            sends.append(
                pltpu.make_async_remote_copy(
                    src_ref=sum_ref.at[it, r],
                    dst_ref=red_ref.at[it, r, spot],
                    send_sem=rsend_sem.at[it, r],
                    recv_sem=rrecv_sem.at[it, r],
                    device_id=partner(r, j),
                    device_id_type=MESH,
                )
            )
        red_ref[it, r, spot] = sum_ref[it, r]
        for send in sends:
            send.start()

    def reduce_wait(it, r):
        _, _, size = rounds[r]
        block = red_ref.at[it, r, pl.ds(0, size - 1)]
        pltpu.make_async_copy(block, block, rrecv_sem.at[it, r]).wait()
        total = red_ref[it, r, 0]
        for j in range(1, size):
            total = total + red_ref[it, r, j]
        return total

    for it in range(ITERS):
        found = gather_tile(
            [lambda row, c=c: ext_ref[c, row : row + 1, :] for c in range(3)], 72, parent_index
        )
        for c in range(3):
            ext_ref[c, 72:74, :] = (
                0.375 * found[c][0:2] + 0.75 * found[c][2:4] - 0.125 * found[c][4:6]
            )
        fields = [lambda row, c=c: ext_ref[c, row : row + 1, :] for c in range(3)]

        def gather_rows(tile, _):
            top = pl.multiple_of(tile * 8, 8)
            for j in range(8):
                columns = slice(j * 128, j * 128 + 128)
                got = gather_tile(fields, EXT_ROWS, cells_ref[pl.ds(top, 8), columns])
                for c in range(3):
                    u_ref[c, pl.ds(top, 8), columns] = got[c]
            return 0

        lax.fori_loop(0, 3, gather_rows, 0)
        for k in range(24, 27):
            index = jnp.concatenate(
                [cells_ref[k : k + 1, s * 128 : s * 128 + 128] for s in range(8)], 0
            )
            got = gather_tile(fields, EXT_ROWS, index)
            for c in range(3):
                for s in range(8):
                    u_ref[c, k : k + 1, s * 128 : s * 128 + 128] = got[c][s : s + 1]

        u = u_ref[...].reshape(96, 1024)
        u_high = u.astype(BF16)
        u_low = (u - u_high.astype(F32)).astype(BF16)
        t = (
            jnp.dot(stiff_high, u_high, preferred_element_type=F32)
            + jnp.dot(stiff_high, u_low, preferred_element_type=F32)
            + jnp.dot(stiff_low, u_high, preferred_element_type=F32)
        ) * weight
        t_ref[...] = t
        bent = jnp.sum(u * t, 0, keepdims=True)
        bent = sum(bent[:, j * 128 : j * 128 + 128] for j in range(8))
        norm = sum(res_ref[c] * ext_ref[c, 0:OWN_ROWS, :] for c in range(3))
        norm = jnp.sum(norm, 0, keepdims=True)
        sum_ref[it, 0] = jnp.concatenate(
            [jnp.broadcast_to(norm, (4, 128)), jnp.broadcast_to(bent, (4, 128))], 0
        )
        reduce_send(it, 0)

        acc_ref[...] = jnp.zeros_like(acc_ref)

        def scatter_step(step, _):
            bands, places, values = [], [], [[], [], []]
            for i in range(STEP_K):
                k = step * STEP_K + i
                bands.append(band_ref[pl.ds(k, 1), :])
                places.append(place_ref[pl.ds(k, 1), :])
                for c in range(3):
                    values[c].append(t_ref[pl.ds(c * 32 + k, 1), :])
            acc_ref[...] += spread_dot(
                jnp.concatenate(bands, 1),
                jnp.concatenate(places, 1),
                [jnp.concatenate(v, 1) for v in values],
            )
            return 0

        steps = 27 // STEP_K
        marks = [steps * i // len(rounds) for i in range(len(rounds) + 1)]
        for r in range(len(rounds)):
            if r > 0:
                sum_ref[it, r] = reduce_wait(it, r - 1)
                reduce_send(it, r)
            lax.fori_loop(marks[r], marks[r + 1], scatter_step, 0)

        hanging = [extra_part(acc_ref, c)[4:5] for c in range(3)]
        fold = spread_dot(
            parent_band,
            parent_place,
            [jnp.concatenate([0.375 * h, 0.75 * h, -0.125 * h], 1) for h in hanging],
        )
        copied = []
        for c in range(3):
            own = own_part(acc_ref, c) + own_part(fold, c)
            part_ref[c, 0:32, :] = own[:, 0:128]
            part_ref[c, 32:64, :] = own[:, 128:256]
            copied.append((extra_part(acc_ref, c) + extra_part(fold, c))[0:4])
        outgoing = gather_tile(
            [lambda row, c=c: part_ref[c, row : row + 1, :] for c in range(3)],
            OWN_ROWS,
            shared_index,
        )
        number = it + 1
        for side in range(2):
            for c in range(3):
                send_ref[number, side, c, 0:4, :] = outgoing[c][side * 4 : side * 4 + 4]
                send_ref[number, side, c, 4:8, :] = copied[c][:, side * 128 : side * 128 + 128]
        copies = exchange(number)
        total = reduce_wait(it, len(rounds) - 1)
        norm = jnp.sum(total[0:1], 1, keepdims=True)
        bent = jnp.sum(total[4:5], 1, keepdims=True)
        step = norm / bent
        for copy in copies:
            copy.wait()
        back = []
        for c in range(3):
            rows = [
                recv_ref[number, side, c, 4 + q : 5 + q, :] * has[side]
                for side in range(2)
                for q in range(4)
            ]
            back.append(jnp.concatenate(rows, 1))
        returned = spread_dot(shared_band, shared_place, back, extra=False)
        for c in range(3):
            add = own_part(returned, c)
            search = ext_ref[c, 0:OWN_ROWS, :]
            image = part_ref[c] + jnp.concatenate([add[:, 0:128], add[:, 128:256]], 0)
            sol_ref[c] = sol_ref[c] + step * search
            residual = res_ref[c] - step * image
            res_ref[c] = residual
            if it + 1 < ITERS:
                ext_ref[c, 0:OWN_ROWS, :] = pre_ref[...] * residual
                for side in range(2):
                    own = slice(side * 4, side * 4 + 4)
                    image = recv_ref[number, side, c, 0:4, :] + send_ref[number, side, c, 4:8, :]
                    gres_ref[c, own, :] = gres_ref[c, own, :] - step * image
                ext_ref[c, OWN_ROWS : OWN_ROWS + 8, :] = gpre_ref[...] * gres_ref[c]

    for it in range(ITERS):
        for r, (_, _, size) in enumerate(rounds):
            block = red_ref.at[it, r, pl.ds(0, size - 1)]
            pltpu.make_async_copy(block, block, rsend_sem.at[it, r]).wait()


def make_local(n_grp, n_cur):
    rounds = []
    rest, stride = n_cur, 1
    while rest > 1:
        size = min(8, rest)
        rounds.append(("cur", stride, size))
        stride, rest = stride * size, rest // size
    if n_grp > 1:
        rounds.append(("grp", 1, n_grp))
    widest = max(size for _, _, size in rounds)

    def local(
        right_side, precond, viscosity, stiffness, element_nodes, live, shared, parents
    ):
        vmem = pl.BlockSpec(memory_space=pltpu.VMEM)
        smem = pl.BlockSpec(memory_space=pltpu.SMEM)
        shape = jax.ShapeDtypeStruct((3, OWN_ROWS, 128), F32)
        call = pl.pallas_call(
            functools.partial(kernel, tuple(rounds), (n_grp, n_cur)),
            out_shape=(shape, shape),
            in_specs=[vmem, vmem, vmem, vmem, vmem, smem, vmem, vmem],
            out_specs=(vmem, vmem),
            scratch_shapes=[
                pltpu.VMEM((3, 80, 128), F32),
                pltpu.VMEM((3, 8, 128), F32),
                pltpu.VMEM((8, 128), F32),
                pltpu.VMEM((32, 1024), jnp.int32),
                pltpu.VMEM((32, 1024), jnp.int32),
                pltpu.VMEM((3, 32, 1024), F32),
                pltpu.VMEM((96, 1024), F32),
                pltpu.VMEM((240, 256), F32),
                pltpu.VMEM((3, OWN_ROWS, 128), F32),
                pltpu.VMEM((ITERS + 1, 2, 3, 8, 128), F32),
                pltpu.VMEM((ITERS + 1, 2, 3, 8, 128), F32),
                pltpu.VMEM((ITERS, len(rounds), widest, 8, 128), F32),
                pltpu.VMEM((ITERS, len(rounds), 8, 128), F32),
                pltpu.SemaphoreType.DMA((ITERS + 1, 2)),
                pltpu.SemaphoreType.DMA((ITERS + 1, 2)),
                pltpu.SemaphoreType.DMA((ITERS, len(rounds))),
                pltpu.SemaphoreType.DMA((ITERS, len(rounds))),
            ],
            compiler_params=pltpu.CompilerParams(
                collective_id=0, has_side_effects=True, vmem_limit_bytes=48 * 1024 * 1024
            ),
            name="descent",
        )
        sol, res = call(
            right_side.reshape(3, OWN_ROWS, 128),
            precond.reshape(OWN_ROWS, 128),
            viscosity.reshape(1, 1024),
            stiffness,
            element_nodes,
            live,
            shared,
            parents,
        )
        return sol.reshape(3, OWN_ROWS * 128), res.reshape(3, OWN_ROWS * 128)

    return local


def solution(mesh):
    both = ("grp", "cur")
    in_specs = (
        P(None, both),
        P(both),
        P(both),
        P(),
        P(None, both),
        P(both),
        P(None, both),
        P(None, both),
    )
    out_specs = (P(None, both), P(None, both))
    return jax.shard_map(
        make_local(mesh.shape["grp"], mesh.shape["cur"]),
        mesh=mesh,
        in_specs=in_specs,
        out_specs=out_specs,
        check_vma=False,
    )
```

```python
import functools

import jax
import jax.numpy as jnp
from jax import lax
from jax.experimental import pallas as pl
from jax.experimental.pallas import tpu as pltpu
from jax.sharding import PartitionSpec as P

ITERS = 3
F32 = jnp.float32
BF16 = jnp.bfloat16
MESH = pl.DeviceIdType.MESH
OWN_ROWS = 64
EXT_ROWS = 74
CHUNKS = 8
NODES = 28


def take(src, lanes):
    return jnp.take_along_axis(src, lanes, axis=1, mode="promise_in_bounds")


def gather_tile(fields, row_count, index):
    lanes = index & 127
    rows = index >> 7
    found = [jnp.zeros((8, 128), F32) for _ in fields]
    for row in range(row_count):
        hit = rows == row
        for i, field in enumerate(fields):
            line = jnp.broadcast_to(field(row), (8, 128))
            found[i] = jnp.where(hit, take(line, lanes), found[i])
    return found


def folded(index):
    row = index >> 7
    lane = index & 127
    own = row < 64
    hang = row >= 72
    band = jnp.where(own, row & 31, jnp.where(hang, 36, 32 + (row & 3)))
    half = jnp.where(own, row >> 5, jnp.where(hang, row & 1, (row >> 2) & 1))
    return band, half * 128 + lane


def pieces(row):
    high = row.astype(BF16)
    low = (row - high.astype(F32)).astype(BF16)
    return high, low


def spread_dot(band, place, values, extra=True):
    n = band.shape[1]
    band16 = band.astype(jnp.int16)
    place16 = place.astype(jnp.int16)
    zero = jnp.zeros((16, n), BF16)
    one = jnp.ones((256, n), BF16)
    hot = jnp.where(
        lax.broadcasted_iota(jnp.int16, (256, n), 0) == place16, one, jnp.zeros((256, n), BF16)
    )
    line = lax.broadcasted_iota(jnp.int16, (16, n), 0)
    hit0 = line == band16
    hit1 = (line + jnp.int16(16)) == band16
    parts = []
    tails = []
    if extra:
        first = line < jnp.int16(8)
        hit2 = jnp.where(first, line, line - jnp.int16(8)) == (band16 - jnp.int16(32))
    for value in values:
        high, low = pieces(value)
        high = jnp.broadcast_to(high, (16, n))
        low = jnp.broadcast_to(low, (16, n))
        for piece in (high, low):
            parts.append(jnp.where(hit0, piece, zero))
            parts.append(jnp.where(hit1, piece, zero))
        if extra:
            tails.append(jnp.where(hit2, jnp.where(first, high, low), zero))
    left = jnp.concatenate(parts + tails, 0)
    return lax.dot_general(left, hot, (((1,), (1,)), ((), ())), preferred_element_type=F32)


def own_part(total, c):
    return total[c * 64 : c * 64 + 32] + total[c * 64 + 32 : c * 64 + 64]


def extra_part(total, c):
    return total[192 + c * 16 : 200 + c * 16] + total[200 + c * 16 : 208 + c * 16]


def chunk_dot(band_ref, place_ref, piece_ref, columns):
    zero = jnp.zeros((16, 128), BF16)
    one = jnp.ones((16, 128), BF16)
    line = lax.broadcasted_iota(jnp.int16, (16, 128), 0)
    lines = [line + jnp.int16(16 * i) for i in range(16)]
    first = line < jnp.int16(8)
    beyond = jnp.where(first, line, line - jnp.int16(8)) + jnp.int16(32)
    hots, lefts = [], []
    for k in range(NODES):
        band = jnp.broadcast_to(band_ref[k : k + 1, columns], (16, 128)).astype(jnp.int16)
        place = jnp.broadcast_to(place_ref[k : k + 1, columns], (16, 128)).astype(jnp.int16)
        hots.append(jnp.concatenate([jnp.where(at == place, one, zero) for at in lines], 0))
        hits = [lines[0] == band, lines[1] == band]
        hit_beyond = beyond == band
        parts, tails = [], []
        for c in range(3):
            row = c * 32 + k
            pair = [
                jnp.broadcast_to(piece_ref[p, row : row + 1, :], (16, 128)).astype(BF16)
                for p in range(2)
            ]
            parts += [jnp.where(hit, piece, zero) for piece in pair for hit in hits]
            tails.append(jnp.where(hit_beyond, jnp.where(first, pair[0], pair[1]), zero))
        lefts.append(jnp.concatenate(parts + tails, 0))
    return lax.dot_general(
        jnp.concatenate(lefts, 1),
        jnp.concatenate(hots, 1),
        (((1,), (1,)), ((), ())),
        preferred_element_type=F32,
    )


def kernel(
    rounds,
    sizes,
    rhs_ref,
    pre_ref,
    visc_ref,
    stiff_ref,
    cells_ref,
    live_ref,
    shared_ref,
    parents_ref,
    sol_ref,
    res_ref,
    ext_ref,
    search_ref,
    image_ref,
    gimage_ref,
    gpre_ref,
    weight_ref,
    matrix_ref,
    band_ref,
    place_ref,
    u_ref,
    piece_ref,
    acc_ref,
    part_ref,
    step_ref,
    send_ref,
    recv_ref,
    red_ref,
    sum_ref,
    send_sem,
    recv_sem,
    rsend_sem,
    rrecv_sem,
):
    n_grp, n_cur = sizes
    devices = n_grp * n_cur
    my_grp = lax.axis_index("grp")
    my_cur = lax.axis_index("cur")
    me = my_grp * n_cur + my_cur

    def ring(offset):
        other = lax.rem(me + offset + devices, devices)
        return {"grp": other // n_cur, "cur": lax.rem(other, n_cur)}

    def my_place(r):
        axis, stride, size = rounds[r]
        mine = my_cur if axis == "cur" else my_grp
        return lax.rem(mine // stride, size)

    def partner(r, j):
        axis, stride, size = rounds[r]
        mine = my_cur if axis == "cur" else my_grp
        place = my_place(r)
        return {axis: mine + (lax.rem(place + j, size) - place) * stride}

    barrier = pltpu.get_barrier_semaphore()
    targets = [ring(-1), ring(1)]
    for r, (_, _, size) in enumerate(rounds):
        targets += [partner(r, j) for j in range(1, size)]
    for target in targets:
        pl.semaphore_signal(barrier, inc=1, device_id=target, device_id_type=MESH)

    band_ref[24:32, :] = jnp.zeros((8, 1024), jnp.int32)
    place_ref[24:32, :] = jnp.zeros((8, 1024), jnp.int32)
    band, place = folded(cells_ref[...])
    band_ref[0:27, :] = band
    place_ref[0:27, :] = place
    shared_index = jnp.concatenate(
        [shared_ref[j : j + 1, q * 128 : (q + 1) * 128] for j in range(2) for q in range(4)], 0
    )
    parent_rows = [parents_ref[p : p + 1, q * 128 : (q + 1) * 128] for p in range(3) for q in range(2)]
    parent_index = jnp.concatenate(parent_rows + parent_rows[:2], 0)
    shared_band, shared_place = folded(
        jnp.concatenate([shared_ref[0:1, :], shared_ref[1:2, :]], 1)
    )
    parent_band, parent_place = folded(
        jnp.concatenate([parents_ref[p : p + 1, :] for p in range(3)], 1)
    )
    slot = lax.broadcasted_iota(jnp.int32, (1, 1024), 1)
    weight_ref[...] = jnp.where(slot < live_ref[0], visc_ref[...], 0.0)
    at = lax.broadcasted_iota(jnp.int32, (96, 81), 0)
    want = jnp.where((at & 31) < 27, (at >> 5) * 27 + (at & 31), -1)
    pick = jnp.where(want == lax.broadcasted_iota(jnp.int32, (96, 81), 1), 1.0, 0.0).astype(BF16)

    def padded(part):
        rows = lax.dot_general(pick, part, (((1,), (1,)), ((), ())), preferred_element_type=F32)
        return lax.dot_general(
            rows.astype(BF16), pick, (((1,), (1,)), ((), ())), preferred_element_type=F32
        ).astype(BF16)

    stiff = stiff_ref[...]
    stiff_high = stiff.astype(BF16)
    matrix_ref[0] = padded(stiff_high)
    matrix_ref[1] = padded((stiff - stiff_high.astype(F32)).astype(BF16))

    u_ref[...] = jnp.zeros_like(u_ref)
    gimage_ref[...] = jnp.zeros_like(gimage_ref)
    step_ref[0] = jnp.zeros((8, 128), F32)
    step_ref[1] = jnp.full((8, 128), -1.0, F32)
    for c in range(3):
        res_ref[c] = rhs_ref[c]
        sol_ref[c] = jnp.zeros((OWN_ROWS, 128), F32)
        image_ref[c] = jnp.zeros((OWN_ROWS, 128), F32)
        search = pre_ref[...] * rhs_ref[c]
        ext_ref[c, 0:OWN_ROWS, :] = search
        search_ref[c] = search

    def exchange(number):
        copies = []
        for side, offset in ((0, -1), (1, 1)):
            copies.append(
                pltpu.make_async_remote_copy(
                    src_ref=send_ref.at[number, side],
                    dst_ref=recv_ref.at[number, 1 - side],
                    send_sem=send_sem.at[number, side],
                    recv_sem=recv_sem.at[number, 1 - side],
                    device_id=ring(offset),
                    device_id_type=MESH,
                )
            )
        for copy in copies:
            copy.start()
        return copies

    outgoing = gather_tile(
        [lambda row, c=c: rhs_ref[c, row : row + 1, :] for c in range(3)]
        + [lambda row: pre_ref[row : row + 1, :]],
        OWN_ROWS,
        shared_index,
    )
    for side in range(2):
        for c in range(3):
            send_ref[0, side, c, 0:4, :] = outgoing[c][side * 4 : side * 4 + 4]
            send_ref[0, side, c, 4:8, :] = outgoing[3][side * 4 : side * 4 + 4]
    pl.semaphore_wait(barrier, len(targets))
    copies = exchange(0)
    for copy in copies:
        copy.wait()
    has = [
        jnp.where(me > 0, 1.0, 0.0).astype(F32),
        jnp.where(me < devices - 1, 1.0, 0.0).astype(F32),
    ]
    for side in range(2):
        own = slice(side * 4, side * 4 + 4)
        gpre_ref[own, :] = recv_ref[0, side, 0, 4:8, :] * has[side]
        for c in range(3):
            ext_ref[c, OWN_ROWS + side * 4 : OWN_ROWS + side * 4 + 4, :] = (
                gpre_ref[own, :] * recv_ref[0, side, c, 0:4, :]
            )

    def reduce_send(it, r):
        _, _, size = rounds[r]
        spot = my_place(r)
        red_ref[it, r, spot] = sum_ref[it, r]
        for j in range(1, size):
            pltpu.make_async_remote_copy(
                src_ref=sum_ref.at[it, r],
                dst_ref=red_ref.at[it, r, spot],
                send_sem=rsend_sem.at[it, r],
                recv_sem=rrecv_sem.at[it, r],
                device_id=partner(r, j),
                device_id_type=MESH,
            ).start()

    def reduce_wait(it, r):
        _, _, size = rounds[r]
        block = red_ref.at[it, r, pl.ds(0, size - 1)]
        pltpu.make_async_copy(block, block, rrecv_sem.at[it, r]).wait()
        total = red_ref[it, r, 0]
        for j in range(1, size):
            total = total + red_ref[it, r, j]
        return total

    def reduce_step(it, r):
        sum_ref[it, r] = reduce_wait(it, r - 1)
        reduce_send(it, r)

    def reduce_end(it):
        total = reduce_wait(it, len(rounds) - 1)
        norm = jnp.sum(total[0:1], 1, keepdims=True)
        bent = jnp.sum(total[4:5], 1, keepdims=True)
        step = jnp.broadcast_to(norm / bent, (8, 128))
        step_ref[0] = step
        step_ref[1] = step

    fields = [lambda row, c=c: ext_ref[c, row : row + 1, :] for c in range(3)]
    marks = [1 + (6 * r) // len(rounds) for r in range(len(rounds))]

    def columns_of(chunk):
        if isinstance(chunk, int):
            return pl.ds(chunk * 128, 128)
        return pl.ds(pl.multiple_of(chunk * 128, 128), 128)

    def gather(chunk):
        for top in range(0, 24, 8):
            got = gather_tile(fields, EXT_ROWS, cells_ref[top : top + 8, columns_of(chunk)])
            for c in range(3):
                u_ref[chunk, c, top : top + 8, :] = got[c]

    def element(chunk):
        u = u_ref[chunk].reshape(96, 128)
        u_high = u.astype(BF16)
        u_low = (u - u_high.astype(F32)).astype(BF16)
        high, low = matrix_ref[0], matrix_ref[1]
        t = (
            jnp.dot(high, u_high, preferred_element_type=F32)
            + jnp.dot(high, u_low, preferred_element_type=F32)
            + jnp.dot(low, u_high, preferred_element_type=F32)
        ) * weight_ref[0:1, columns_of(chunk)]
        t_high = t.astype(BF16).astype(F32)
        piece_ref[0] = t_high
        piece_ref[1] = t - t_high

    def scatter(chunk):
        acc_ref[...] += chunk_dot(band_ref, place_ref, piece_ref, columns_of(chunk))

    def iteration(it, _):
        found = gather_tile(fields, 72, parent_index)
        for c in range(3):
            ext_ref[c, 72:74, :] = (
                0.375 * found[c][0:2] + 0.75 * found[c][2:4] - 0.125 * found[c][4:6]
            )
        acc_ref[...] = jnp.zeros_like(acc_ref)
        for k in range(24, 27):
            index = jnp.concatenate(
                [cells_ref[k : k + 1, s * 128 : s * 128 + 128] for s in range(CHUNKS)], 0
            )
            got = gather_tile(fields, EXT_ROWS, index)
            for c in range(3):
                for s in range(CHUNKS):
                    u_ref[s, c, k : k + 1, :] = got[c][s : s + 1]
        gather(0)

        def chunk_step(chunk, _):
            for r in range(1, len(rounds)):

                @pl.when((it > 0) & (chunk == marks[r]))
                def _():
                    reduce_step(it - 1, r)

            element(chunk)
            gather(chunk + 1)
            scatter(chunk)
            return 0

        lax.fori_loop(0, CHUNKS - 1, chunk_step, 0)
        element(CHUNKS - 1)
        scatter(CHUNKS - 1)

        hanging = [extra_part(acc_ref, c)[4:5] for c in range(3)]
        fold = spread_dot(
            parent_band,
            parent_place,
            [jnp.concatenate([0.375 * h, 0.75 * h, -0.125 * h], 1) for h in hanging],
        )
        copied = []
        for c in range(3):
            own = own_part(acc_ref, c) + own_part(fold, c)
            part_ref[c, 0:32, :] = own[:, 0:128]
            part_ref[c, 32:64, :] = own[:, 128:256]
            copied.append((extra_part(acc_ref, c) + extra_part(fold, c))[0:4])
        outgoing = gather_tile(
            [lambda row, c=c: part_ref[c, row : row + 1, :] for c in range(3)],
            OWN_ROWS,
            shared_index,
        )
        number = it + 1
        for side in range(2):
            for c in range(3):
                send_ref[number, side, c, 0:4, :] = outgoing[c][side * 4 : side * 4 + 4]
                send_ref[number, side, c, 4:8, :] = copied[c][:, side * 128 : side * 128 + 128]
        copies = exchange(number)

        @pl.when(it > 0)
        def _():
            reduce_end(it - 1)

        for copy in copies:
            copy.wait()
        step = step_ref[0, 0:1, :]
        turn = step_ref[1, 0:1, :]
        back = []
        for c in range(3):
            rows = [
                recv_ref[number, side, c, 4 + q : 5 + q, :] * has[side]
                for side in range(2)
                for q in range(4)
            ]
            back.append(jnp.concatenate(rows, 1))
        returned = spread_dot(shared_band, shared_place, back, extra=False)
        norm = jnp.zeros((OWN_ROWS, 128), F32)
        bent = jnp.zeros((OWN_ROWS, 128), F32)
        for c in range(3):
            add = own_part(returned, c)
            fresh = part_ref[c] + jnp.concatenate([add[:, 0:128], add[:, 128:256]], 0)
            sol_ref[c] = sol_ref[c] + step * search_ref[c]
            residual = res_ref[c] - step * image_ref[c]
            res_ref[c] = residual
            search = pre_ref[...] * residual
            search_ref[c] = search
            image = image_ref[c] - turn * fresh
            image_ref[c] = image
            ext_ref[c, 0:OWN_ROWS, :] = pre_ref[...] * image
            norm = norm + residual * search
            bent = bent + search * image
            ghost = jnp.concatenate(
                [
                    recv_ref[number, side, c, 0:4, :] + send_ref[number, side, c, 4:8, :]
                    for side in range(2)
                ],
                0,
            )
            ghost = gimage_ref[c] - turn * ghost
            gimage_ref[c] = ghost
            ext_ref[c, OWN_ROWS : OWN_ROWS + 8, :] = gpre_ref[...] * ghost
        sum_ref[it, 0] = jnp.concatenate(
            [
                jnp.broadcast_to(jnp.sum(norm, 0, keepdims=True), (4, 128)),
                jnp.broadcast_to(jnp.sum(bent, 0, keepdims=True), (4, 128)),
            ],
            0,
        )
        reduce_send(it, 0)
        return 0

    lax.fori_loop(0, ITERS, iteration, 0)
    for r in range(1, len(rounds)):
        reduce_step(ITERS - 1, r)
    reduce_end(ITERS - 1)
    step = step_ref[0, 0:1, :]
    for c in range(3):
        sol_ref[c] = sol_ref[c] + step * search_ref[c]
        res_ref[c] = res_ref[c] - step * image_ref[c]
    for it in range(ITERS):
        for r, (_, _, size) in enumerate(rounds):
            block = red_ref.at[it, r, pl.ds(0, size - 1)]
            pltpu.make_async_copy(block, block, rsend_sem.at[it, r]).wait()


def make_local(n_grp, n_cur):
    rounds = []
    rest, stride = n_cur, 1
    while rest > 1:
        size = min(8, rest)
        rounds.append(("cur", stride, size))
        stride, rest = stride * size, rest // size
    if n_grp > 1:
        rounds.append(("grp", 1, n_grp))
    widest = max(size for _, _, size in rounds)

    def local(
        right_side, precond, viscosity, stiffness, element_nodes, live, shared, parents
    ):
        vmem = pl.BlockSpec(memory_space=pltpu.VMEM)
        smem = pl.BlockSpec(memory_space=pltpu.SMEM)
        shape = jax.ShapeDtypeStruct((3, OWN_ROWS, 128), F32)
        call = pl.pallas_call(
            functools.partial(kernel, tuple(rounds), (n_grp, n_cur)),
            out_shape=(shape, shape),
            in_specs=[vmem, vmem, vmem, vmem, vmem, smem, vmem, vmem],
            out_specs=(vmem, vmem),
            scratch_shapes=[
                pltpu.VMEM((3, 80, 128), F32),
                pltpu.VMEM((3, OWN_ROWS, 128), F32),
                pltpu.VMEM((3, OWN_ROWS, 128), F32),
                pltpu.VMEM((3, 8, 128), F32),
                pltpu.VMEM((8, 128), F32),
                pltpu.VMEM((1, 1024), F32),
                pltpu.VMEM((2, 96, 96), BF16),
                pltpu.VMEM((32, 1024), jnp.int32),
                pltpu.VMEM((32, 1024), jnp.int32),
                pltpu.VMEM((CHUNKS, 3, 32, 128), F32),
                pltpu.VMEM((2, 96, 128), F32),
                pltpu.VMEM((240, 256), F32),
                pltpu.VMEM((3, OWN_ROWS, 128), F32),
                pltpu.VMEM((2, 8, 128), F32),
                pltpu.VMEM((ITERS + 1, 2, 3, 8, 128), F32),
                pltpu.VMEM((ITERS + 1, 2, 3, 8, 128), F32),
                pltpu.VMEM((ITERS, len(rounds), widest, 8, 128), F32),
                pltpu.VMEM((ITERS, len(rounds), 8, 128), F32),
                pltpu.SemaphoreType.DMA((ITERS + 1, 2)),
                pltpu.SemaphoreType.DMA((ITERS + 1, 2)),
                pltpu.SemaphoreType.DMA((ITERS, len(rounds))),
                pltpu.SemaphoreType.DMA((ITERS, len(rounds))),
            ],
            compiler_params=pltpu.CompilerParams(
                collective_id=0, has_side_effects=True, vmem_limit_bytes=48 * 1024 * 1024
            ),
            name="descent",
        )
        sol, res = call(
            right_side.reshape(3, OWN_ROWS, 128),
            precond.reshape(OWN_ROWS, 128),
            viscosity.reshape(1, 1024),
            stiffness,
            element_nodes,
            live,
            shared,
            parents,
        )
        return sol.reshape(3, OWN_ROWS * 128), res.reshape(3, OWN_ROWS * 128)

    return local


def solution(mesh):
    both = ("grp", "cur")
    in_specs = (
        P(None, both),
        P(both),
        P(both),
        P(),
        P(None, both),
        P(both),
        P(None, both),
        P(None, both),
    )
    out_specs = (P(None, both), P(None, both))
    return jax.shard_map(
        make_local(mesh.shape["grp"], mesh.shape["cur"]),
        mesh=mesh,
        in_specs=in_specs,
        out_specs=out_specs,
        check_vma=False,
    )
```

```python
import functools

import jax
import jax.numpy as jnp
from jax import lax
from jax.experimental import pallas as pl
from jax.experimental.pallas import tpu as pltpu
from jax.sharding import PartitionSpec as P

ITERS = 3
F32 = jnp.float32
BF16 = jnp.bfloat16
MESH = pl.DeviceIdType.MESH
OWN_ROWS = 64
EXT_ROWS = 74
CHUNKS = 8
NODES = 28


def take(src, lanes):
    return jnp.take_along_axis(src, lanes, axis=1, mode="promise_in_bounds")


def gather_tile(fields, row_count, index):
    lanes = index & 127
    rows = index >> 7
    found = [jnp.zeros((8, 128), F32) for _ in fields]
    for row in range(row_count):
        hit = rows == row
        for i, field in enumerate(fields):
            line = jnp.broadcast_to(field(row), (8, 128))
            found[i] = jnp.where(hit, take(line, lanes), found[i])
    return found


def folded(index):
    row = index >> 7
    lane = index & 127
    own = row < 64
    hang = row >= 72
    band = jnp.where(own, row & 31, jnp.where(hang, 36, 32 + (row & 3)))
    half = jnp.where(own, row >> 5, jnp.where(hang, row & 1, (row >> 2) & 1))
    return band, half * 128 + lane


def pieces(row):
    high = row.astype(BF16)
    low = (row - high.astype(F32)).astype(BF16)
    return high, low


def spread_dot(band, place, values, extra=True):
    n = band.shape[1]
    band16 = band.astype(jnp.int16)
    place16 = place.astype(jnp.int16)
    zero = jnp.zeros((16, n), BF16)
    one = jnp.ones((256, n), BF16)
    hot = jnp.where(
        lax.broadcasted_iota(jnp.int16, (256, n), 0) == place16, one, jnp.zeros((256, n), BF16)
    )
    line = lax.broadcasted_iota(jnp.int16, (16, n), 0)
    hit0 = line == band16
    hit1 = (line + jnp.int16(16)) == band16
    parts = []
    tails = []
    if extra:
        first = line < jnp.int16(8)
        hit2 = jnp.where(first, line, line - jnp.int16(8)) == (band16 - jnp.int16(32))
    for value in values:
        high, low = pieces(value)
        high = jnp.broadcast_to(high, (16, n))
        low = jnp.broadcast_to(low, (16, n))
        for piece in (high, low):
            parts.append(jnp.where(hit0, piece, zero))
            parts.append(jnp.where(hit1, piece, zero))
        if extra:
            tails.append(jnp.where(hit2, jnp.where(first, high, low), zero))
    left = jnp.concatenate(parts + tails, 0)
    return lax.dot_general(left, hot, (((1,), (1,)), ((), ())), preferred_element_type=F32)


def own_part(total, c):
    return total[c * 64 : c * 64 + 32] + total[c * 64 + 32 : c * 64 + 64]


def extra_part(total, c):
    return total[192 + c * 16 : 200 + c * 16] + total[200 + c * 16 : 208 + c * 16]


def chunk_dot(band_ref, place_ref, piece_ref, columns):
    zero = jnp.zeros((16, 128), BF16)
    one = jnp.ones((16, 128), BF16)
    line = lax.broadcasted_iota(jnp.int16, (16, 128), 0)
    lines = [line + jnp.int16(16 * i) for i in range(16)]
    first = line < jnp.int16(8)
    beyond = jnp.where(first, line, line - jnp.int16(8)) + jnp.int16(32)
    hots, lefts = [], []
    for k in range(NODES):
        band = jnp.broadcast_to(band_ref[k : k + 1, columns], (16, 128)).astype(jnp.int16)
        place = jnp.broadcast_to(place_ref[k : k + 1, columns], (16, 128)).astype(jnp.int16)
        hots.append(jnp.concatenate([jnp.where(at == place, one, zero) for at in lines], 0))
        hits = [lines[0] == band, lines[1] == band]
        hit_beyond = beyond == band
        parts, tails = [], []
        for c in range(3):
            row = c * 32 + k
            pair = [
                jnp.broadcast_to(piece_ref[p, row : row + 1, :], (16, 128)).astype(BF16)
                for p in range(2)
            ]
            parts += [jnp.where(hit, piece, zero) for piece in pair for hit in hits]
            tails.append(jnp.where(hit_beyond, jnp.where(first, pair[0], pair[1]), zero))
        lefts.append(jnp.concatenate(parts + tails, 0))
    return lax.dot_general(
        jnp.concatenate(lefts, 1),
        jnp.concatenate(hots, 1),
        (((1,), (1,)), ((), ())),
        preferred_element_type=F32,
    )


def kernel(
    rounds,
    sizes,
    rhs_ref,
    pre_ref,
    visc_ref,
    stiff_ref,
    cells_ref,
    live_ref,
    shared_ref,
    parents_ref,
    sol_ref,
    res_ref,
    ext_ref,
    search_ref,
    image_ref,
    gimage_ref,
    gres_ref,
    gpre_ref,
    weight_ref,
    matrix_ref,
    band_ref,
    place_ref,
    u_ref,
    piece_ref,
    acc_ref,
    part_ref,
    step_ref,
    send_ref,
    recv_ref,
    red_ref,
    sum_ref,
    send_sem,
    recv_sem,
    rsend_sem,
    rrecv_sem,
):
    n_grp, n_cur = sizes
    devices = n_grp * n_cur
    my_grp = lax.axis_index("grp")
    my_cur = lax.axis_index("cur")
    me = my_grp * n_cur + my_cur

    def ring(offset):
        other = lax.rem(me + offset + devices, devices)
        return {"grp": other // n_cur, "cur": lax.rem(other, n_cur)}

    def my_place(r):
        axis, stride, size = rounds[r]
        mine = my_cur if axis == "cur" else my_grp
        return lax.rem(mine // stride, size)

    def partner(r, j):
        axis, stride, size = rounds[r]
        mine = my_cur if axis == "cur" else my_grp
        place = my_place(r)
        return {axis: mine + (lax.rem(place + j, size) - place) * stride}

    barrier = pltpu.get_barrier_semaphore()
    targets = [ring(-1), ring(1)]
    for r, (_, _, size) in enumerate(rounds):
        targets += [partner(r, j) for j in range(1, size)]
    for target in targets:
        pl.semaphore_signal(barrier, inc=1, device_id=target, device_id_type=MESH)

    band_ref[24:32, :] = jnp.zeros((8, 1024), jnp.int32)
    place_ref[24:32, :] = jnp.zeros((8, 1024), jnp.int32)
    band, place = folded(cells_ref[...])
    band_ref[0:27, :] = band
    place_ref[0:27, :] = place
    shared_index = jnp.concatenate(
        [shared_ref[j : j + 1, q * 128 : (q + 1) * 128] for j in range(2) for q in range(4)], 0
    )
    parent_rows = [parents_ref[p : p + 1, q * 128 : (q + 1) * 128] for p in range(3) for q in range(2)]
    parent_index = jnp.concatenate(parent_rows + parent_rows[:2], 0)
    shared_band, shared_place = folded(
        jnp.concatenate([shared_ref[0:1, :], shared_ref[1:2, :]], 1)
    )
    parent_band, parent_place = folded(
        jnp.concatenate([parents_ref[p : p + 1, :] for p in range(3)], 1)
    )
    slot = lax.broadcasted_iota(jnp.int32, (1, 1024), 1)
    weight_ref[...] = jnp.where(slot < live_ref[0], visc_ref[...], 0.0)
    at = lax.broadcasted_iota(jnp.int32, (96, 81), 0)
    want = jnp.where((at & 31) < 27, (at >> 5) * 27 + (at & 31), -1)
    pick = jnp.where(want == lax.broadcasted_iota(jnp.int32, (96, 81), 1), 1.0, 0.0).astype(BF16)

    def padded(part):
        rows = lax.dot_general(pick, part, (((1,), (1,)), ((), ())), preferred_element_type=F32)
        return lax.dot_general(
            rows.astype(BF16), pick, (((1,), (1,)), ((), ())), preferred_element_type=F32
        ).astype(BF16)

    stiff = stiff_ref[...]
    stiff_high = stiff.astype(BF16)
    matrix_ref[0] = padded(stiff_high)
    matrix_ref[1] = padded((stiff - stiff_high.astype(F32)).astype(BF16))

    u_ref[...] = jnp.zeros_like(u_ref)
    gimage_ref[...] = jnp.zeros_like(gimage_ref)
    step_ref[0] = jnp.zeros((8, 128), F32)
    step_ref[1] = jnp.full((8, 128), -1.0, F32)
    for c in range(3):
        res_ref[c] = rhs_ref[c]
        sol_ref[c] = jnp.zeros((OWN_ROWS, 128), F32)
        image_ref[c] = jnp.zeros((OWN_ROWS, 128), F32)
        search = pre_ref[...] * rhs_ref[c]
        ext_ref[c, 0:OWN_ROWS, :] = search
        search_ref[c] = search

    def exchange(number):
        copies = []
        for side, offset in ((0, -1), (1, 1)):
            copies.append(
                pltpu.make_async_remote_copy(
                    src_ref=send_ref.at[number, side],
                    dst_ref=recv_ref.at[number, 1 - side],
                    send_sem=send_sem.at[number, side],
                    recv_sem=recv_sem.at[number, 1 - side],
                    device_id=ring(offset),
                    device_id_type=MESH,
                )
            )
        for copy in copies:
            copy.start()
        return copies

    outgoing = gather_tile(
        [lambda row, c=c: rhs_ref[c, row : row + 1, :] for c in range(3)]
        + [lambda row: pre_ref[row : row + 1, :]],
        OWN_ROWS,
        shared_index,
    )
    for side in range(2):
        for c in range(3):
            send_ref[0, side, c, 0:4, :] = outgoing[c][side * 4 : side * 4 + 4]
            send_ref[0, side, c, 4:8, :] = outgoing[3][side * 4 : side * 4 + 4]
    pl.semaphore_wait(barrier, len(targets))
    copies = exchange(0)
    for copy in copies:
        copy.wait()
    has = [
        jnp.where(me > 0, 1.0, 0.0).astype(F32),
        jnp.where(me < devices - 1, 1.0, 0.0).astype(F32),
    ]
    for side in range(2):
        own = slice(side * 4, side * 4 + 4)
        gpre_ref[own, :] = recv_ref[0, side, 0, 4:8, :] * has[side]
        for c in range(3):
            ghost = recv_ref[0, side, c, 0:4, :]
            gres_ref[c, own, :] = ghost
            ext_ref[c, OWN_ROWS + side * 4 : OWN_ROWS + side * 4 + 4, :] = gpre_ref[own, :] * ghost

    def reduce_send(it, r):
        _, _, size = rounds[r]
        spot = my_place(r)
        red_ref[it, r, spot] = sum_ref[it, r]
        for j in range(1, size):
            pltpu.make_async_remote_copy(
                src_ref=sum_ref.at[it, r],
                dst_ref=red_ref.at[it, r, spot],
                send_sem=rsend_sem.at[it, r],
                recv_sem=rrecv_sem.at[it, r],
                device_id=partner(r, j),
                device_id_type=MESH,
            ).start()

    def reduce_wait(it, r):
        _, _, size = rounds[r]
        block = red_ref.at[it, r, pl.ds(0, size - 1)]
        pltpu.make_async_copy(block, block, rrecv_sem.at[it, r]).wait()
        total = red_ref[it, r, 0]
        for j in range(1, size):
            total = total + red_ref[it, r, j]
        return total

    def reduce_step(it, r):
        sum_ref[it, r] = reduce_wait(it, r - 1)
        reduce_send(it, r)

    def reduce_end(it):
        total = reduce_wait(it, len(rounds) - 1)
        norm = jnp.sum(total[0:1], 1, keepdims=True)
        bent = jnp.sum(total[4:5], 1, keepdims=True)
        step = jnp.broadcast_to(norm / bent, (8, 128))
        step_ref[0] = step
        step_ref[1] = step

    fields = [lambda row, c=c: ext_ref[c, row : row + 1, :] for c in range(3)]
    marks = [2 * r - 1 for r in range(len(rounds))]

    def columns_of(chunk):
        if isinstance(chunk, int):
            return pl.ds(chunk * 128, 128)
        return pl.ds(pl.multiple_of(chunk * 128, 128), 128)

    def gather(chunk):
        for top in range(0, 24, 8):
            got = gather_tile(fields, EXT_ROWS, cells_ref[top : top + 8, columns_of(chunk)])
            for c in range(3):
                u_ref[chunk, c, top : top + 8, :] = got[c]

    def element(chunk):
        u = u_ref[chunk].reshape(96, 128)
        u_high = u.astype(BF16)
        u_low = (u - u_high.astype(F32)).astype(BF16)
        high, low = matrix_ref[0], matrix_ref[1]
        t = (
            jnp.dot(high, u_high, preferred_element_type=F32)
            + jnp.dot(high, u_low, preferred_element_type=F32)
            + jnp.dot(low, u_high, preferred_element_type=F32)
        ) * weight_ref[0:1, columns_of(chunk)]
        t_high = t.astype(BF16).astype(F32)
        piece_ref[0] = t_high
        piece_ref[1] = t - t_high

    def scatter(chunk):
        acc_ref[...] += chunk_dot(band_ref, place_ref, piece_ref, columns_of(chunk))

    def iteration(it, _):
        found = gather_tile(fields, 72, parent_index)
        for c in range(3):
            ext_ref[c, 72:74, :] = (
                0.375 * found[c][0:2] + 0.75 * found[c][2:4] - 0.125 * found[c][4:6]
            )
        acc_ref[...] = jnp.zeros_like(acc_ref)
        for k in range(24, 27):
            index = jnp.concatenate(
                [cells_ref[k : k + 1, s * 128 : s * 128 + 128] for s in range(CHUNKS)], 0
            )
            got = gather_tile(fields, EXT_ROWS, index)
            for c in range(3):
                for s in range(CHUNKS):
                    u_ref[s, c, k : k + 1, :] = got[c][s : s + 1]
        gather(0)

        def chunk_step(chunk, _):
            for r in range(1, len(rounds)):

                @pl.when((it > 0) & (chunk == marks[r]))
                def _():
                    reduce_step(it - 1, r)

            element(chunk)
            gather(chunk + 1)
            scatter(chunk)
            return 0

        lax.fori_loop(0, CHUNKS - 1, chunk_step, 0)
        element(CHUNKS - 1)
        scatter(CHUNKS - 1)

        hanging = [extra_part(acc_ref, c)[4:5] for c in range(3)]
        fold = spread_dot(
            parent_band,
            parent_place,
            [jnp.concatenate([0.375 * h, 0.75 * h, -0.125 * h], 1) for h in hanging],
        )
        copied = []
        for c in range(3):
            own = own_part(acc_ref, c) + own_part(fold, c)
            part_ref[c, 0:32, :] = own[:, 0:128]
            part_ref[c, 32:64, :] = own[:, 128:256]
            copied.append((extra_part(acc_ref, c) + extra_part(fold, c))[0:4])
        outgoing = gather_tile(
            [lambda row, c=c: part_ref[c, row : row + 1, :] for c in range(3)],
            OWN_ROWS,
            shared_index,
        )
        number = it + 1
        for side in range(2):
            for c in range(3):
                send_ref[number, side, c, 0:4, :] = outgoing[c][side * 4 : side * 4 + 4]
                send_ref[number, side, c, 4:8, :] = copied[c][:, side * 128 : side * 128 + 128]
        copies = exchange(number)

        @pl.when(it > 0)
        def _():
            reduce_end(it - 1)

        step = step_ref[0, 0:1, :]
        turn = step_ref[1, 0:1, :]
        norm = jnp.zeros((OWN_ROWS, 128), F32)
        bent = jnp.zeros((OWN_ROWS, 128), F32)
        bent_copies = jnp.zeros((8, 128), F32)
        for c in range(3):
            sol_ref[c] = sol_ref[c] + step * search_ref[c]
            residual = res_ref[c] - step * image_ref[c]
            res_ref[c] = residual
            search = pre_ref[...] * residual
            search_ref[c] = search
            image = image_ref[c] - turn * part_ref[c]
            image_ref[c] = image
            norm = norm + residual * search
            bent = bent + search * image
            ghost = gres_ref[c] - step * gimage_ref[c]
            gres_ref[c] = ghost
            mine = jnp.concatenate([send_ref[number, side, c, 4:8, :] for side in range(2)], 0)
            bent_copies = bent_copies + gpre_ref[...] * ghost * mine
        bent = jnp.sum(bent, 0, keepdims=True) - turn * jnp.sum(bent_copies, 0, keepdims=True)
        sum_ref[it, 0] = jnp.concatenate(
            [
                jnp.broadcast_to(jnp.sum(norm, 0, keepdims=True), (4, 128)),
                jnp.broadcast_to(bent, (4, 128)),
            ],
            0,
        )
        reduce_send(it, 0)

        for copy in copies:
            copy.wait()
        back = []
        for c in range(3):
            rows = [
                recv_ref[number, side, c, 4 + q : 5 + q, :] * has[side]
                for side in range(2)
                for q in range(4)
            ]
            back.append(jnp.concatenate(rows, 1))
        returned = spread_dot(shared_band, shared_place, back, extra=False)
        for c in range(3):
            add = own_part(returned, c)
            image = image_ref[c] - turn * jnp.concatenate([add[:, 0:128], add[:, 128:256]], 0)
            image_ref[c] = image
            ext_ref[c, 0:OWN_ROWS, :] = pre_ref[...] * image
            ghost = jnp.concatenate(
                [
                    recv_ref[number, side, c, 0:4, :] + send_ref[number, side, c, 4:8, :]
                    for side in range(2)
                ],
                0,
            )
            ghost = gimage_ref[c] - turn * ghost
            gimage_ref[c] = ghost
            ext_ref[c, OWN_ROWS : OWN_ROWS + 8, :] = gpre_ref[...] * ghost
        return 0

    lax.fori_loop(0, ITERS, iteration, 0)
    for r in range(1, len(rounds)):
        reduce_step(ITERS - 1, r)
    reduce_end(ITERS - 1)
    step = step_ref[0, 0:1, :]
    for c in range(3):
        sol_ref[c] = sol_ref[c] + step * search_ref[c]
        res_ref[c] = res_ref[c] - step * image_ref[c]
    for it in range(ITERS):
        for r, (_, _, size) in enumerate(rounds):
            block = red_ref.at[it, r, pl.ds(0, size - 1)]
            pltpu.make_async_copy(block, block, rsend_sem.at[it, r]).wait()


def make_local(n_grp, n_cur):
    rounds = []
    rest, stride = n_cur, 1
    while rest > 1:
        size = min(32, rest)
        rounds.append(("cur", stride, size))
        stride, rest = stride * size, rest // size
    if n_grp > 1:
        rounds.append(("grp", 1, n_grp))
    widest = max(size for _, _, size in rounds)

    def local(
        right_side, precond, viscosity, stiffness, element_nodes, live, shared, parents
    ):
        vmem = pl.BlockSpec(memory_space=pltpu.VMEM)
        smem = pl.BlockSpec(memory_space=pltpu.SMEM)
        shape = jax.ShapeDtypeStruct((3, OWN_ROWS, 128), F32)
        call = pl.pallas_call(
            functools.partial(kernel, tuple(rounds), (n_grp, n_cur)),
            out_shape=(shape, shape),
            in_specs=[vmem, vmem, vmem, vmem, vmem, smem, vmem, vmem],
            out_specs=(vmem, vmem),
            scratch_shapes=[
                pltpu.VMEM((3, 80, 128), F32),
                pltpu.VMEM((3, OWN_ROWS, 128), F32),
                pltpu.VMEM((3, OWN_ROWS, 128), F32),
                pltpu.VMEM((3, 8, 128), F32),
                pltpu.VMEM((3, 8, 128), F32),
                pltpu.VMEM((8, 128), F32),
                pltpu.VMEM((1, 1024), F32),
                pltpu.VMEM((2, 96, 96), BF16),
                pltpu.VMEM((32, 1024), jnp.int32),
                pltpu.VMEM((32, 1024), jnp.int32),
                pltpu.VMEM((CHUNKS, 3, 32, 128), F32),
                pltpu.VMEM((2, 96, 128), F32),
                pltpu.VMEM((240, 256), F32),
                pltpu.VMEM((3, OWN_ROWS, 128), F32),
                pltpu.VMEM((2, 8, 128), F32),
                pltpu.VMEM((ITERS + 1, 2, 3, 8, 128), F32),
                pltpu.VMEM((ITERS + 1, 2, 3, 8, 128), F32),
                pltpu.VMEM((ITERS, len(rounds), widest, 8, 128), F32),
                pltpu.VMEM((ITERS, len(rounds), 8, 128), F32),
                pltpu.SemaphoreType.DMA((ITERS + 1, 2)),
                pltpu.SemaphoreType.DMA((ITERS + 1, 2)),
                pltpu.SemaphoreType.DMA((ITERS, len(rounds))),
                pltpu.SemaphoreType.DMA((ITERS, len(rounds))),
            ],
            compiler_params=pltpu.CompilerParams(
                collective_id=0, has_side_effects=True, vmem_limit_bytes=48 * 1024 * 1024
            ),
            name="descent",
        )
        sol, res = call(
            right_side.reshape(3, OWN_ROWS, 128),
            precond.reshape(OWN_ROWS, 128),
            viscosity.reshape(1, 1024),
            stiffness,
            element_nodes,
            live,
            shared,
            parents,
        )
        return sol.reshape(3, OWN_ROWS * 128), res.reshape(3, OWN_ROWS * 128)

    return local


def solution(mesh):
    both = ("grp", "cur")
    in_specs = (
        P(None, both),
        P(both),
        P(both),
        P(),
        P(None, both),
        P(both),
        P(None, both),
        P(None, both),
    )
    out_specs = (P(None, both), P(None, both))
    return jax.shard_map(
        make_local(mesh.shape["grp"], mesh.shape["cur"]),
        mesh=mesh,
        in_specs=in_specs,
        out_specs=out_specs,
        check_vma=False,
    )
```

```python
import functools

import jax
import jax.numpy as jnp
from jax import lax
from jax.experimental import pallas as pl
from jax.experimental.pallas import tpu as pltpu
from jax.sharding import PartitionSpec as P

ITERS = 3
F32 = jnp.float32
BF16 = jnp.bfloat16
MESH = pl.DeviceIdType.MESH
OWN_ROWS = 64
NEAR = slice(64, 80)
GHOSTS = slice(64, 72)
SHARED = slice(72, 80)
EXT_ROWS = 82
EARLY = 3
CHUNKS = 8
NODES = 28


def take(src, lanes):
    return jnp.take_along_axis(src, lanes, axis=1, mode="promise_in_bounds")


def gather_tile(fields, rows, index, found=None):
    lanes = index & 127
    own = index >> 7
    found = list(found) if found else [jnp.zeros((8, 128), F32) for _ in fields]
    for row in rows:
        hit = own == row
        for i, field in enumerate(fields):
            line = jnp.broadcast_to(field(row), (8, 128))
            found[i] = jnp.where(hit, take(line, lanes), found[i])
    return found


def folded(index):
    row = index >> 7
    lane = index & 127
    own = row < 64
    hang = row >= 80
    near = 32 + (row & 3) + jnp.where(row >= 72, 4, 0)
    band = jnp.where(own, row & 31, jnp.where(hang, 40, near))
    half = jnp.where(own, row >> 5, jnp.where(hang, row & 1, (row >> 2) & 1))
    return band, half * 128 + lane


def pieces(row):
    high = row.astype(BF16)
    low = (row - high.astype(F32)).astype(BF16)
    return high, low


def spread_dot(band, place, values, extra=True):
    n = band.shape[1]
    band16 = band.astype(jnp.int16)
    place16 = place.astype(jnp.int16)
    zero = jnp.zeros((16, n), BF16)
    one = jnp.ones((256, n), BF16)
    hot = jnp.where(
        lax.broadcasted_iota(jnp.int16, (256, n), 0) == place16, one, jnp.zeros((256, n), BF16)
    )
    line = lax.broadcasted_iota(jnp.int16, (16, n), 0)
    hit0 = line == band16
    hit1 = (line + jnp.int16(16)) == band16
    parts = []
    tails = []
    if extra:
        first = line < jnp.int16(8)
        hit2 = jnp.where(first, line, line - jnp.int16(8)) == (band16 - jnp.int16(32))
    for value in values:
        high, low = pieces(value)
        high = jnp.broadcast_to(high, (16, n))
        low = jnp.broadcast_to(low, (16, n))
        for piece in (high, low):
            parts.append(jnp.where(hit0, piece, zero))
            parts.append(jnp.where(hit1, piece, zero))
        if extra:
            tails.append(jnp.where(hit2, jnp.where(first, high, low), zero))
    left = jnp.concatenate(parts + tails, 0)
    return lax.dot_general(left, hot, (((1,), (1,)), ((), ())), preferred_element_type=F32)


def own_part(total, c):
    return total[c * 64 : c * 64 + 32] + total[c * 64 + 32 : c * 64 + 64]


def extra_part(total, c):
    return total[192 + c * 16 : 200 + c * 16] + total[200 + c * 16 : 208 + c * 16]


def hang_part(total, c):
    return total[240 + 2 * c : 241 + 2 * c] + total[241 + 2 * c : 242 + 2 * c]


def as_row(block):
    return jnp.concatenate([block[i : i + 1] for i in range(block.shape[0])], 1)


def halves(wide):
    return jnp.concatenate([wide[:, 0:128], wide[:, 128:256]], 0)


def near_rows(wide):
    return jnp.concatenate(
        [wide[0:4, 0:128], wide[0:4, 128:256], wide[4:8, 0:128], wide[4:8, 128:256]], 0
    )


def chunk_dot(band_ref, place_ref, piece_ref, columns):
    zero = jnp.zeros((16, 128), BF16)
    one = jnp.ones((16, 128), BF16)
    line = lax.broadcasted_iota(jnp.int16, (16, 128), 0)
    lines = [line + jnp.int16(16 * i) for i in range(16)]
    first = line < jnp.int16(8)
    beyond = jnp.where(first, line, line - jnp.int16(8)) + jnp.int16(32)
    hots, lefts = [], []
    for k in range(NODES):
        band = jnp.broadcast_to(band_ref[k : k + 1, columns], (16, 128)).astype(jnp.int16)
        place = jnp.broadcast_to(place_ref[k : k + 1, columns], (16, 128)).astype(jnp.int16)
        hots.append(jnp.concatenate([jnp.where(at == place, one, zero) for at in lines], 0))
        hits = [lines[0] == band, lines[1] == band]
        hit_beyond = beyond == band
        parts, tails = [], []
        for c in range(3):
            row = k * 8 + c * 2
            pair = [
                jnp.broadcast_to(piece_ref[row + p : row + p + 1, :], (16, 128)).astype(BF16)
                for p in range(2)
            ]
            parts += [jnp.where(hit, piece, zero) for piece in pair for hit in hits]
            tails.append(jnp.where(hit_beyond, jnp.where(first, pair[0], pair[1]), zero))
        block = piece_ref[k * 8 : k * 8 + 8, :]
        block = jnp.concatenate([block, jnp.zeros((8, 128), F32)], 0).astype(BF16)
        tails.append(jnp.where(band == jnp.int16(40), block, zero))
        lefts.append(jnp.concatenate(parts + tails, 0))
    return lax.dot_general(
        jnp.concatenate(lefts, 1),
        jnp.concatenate(hots, 1),
        (((1,), (1,)), ((), ())),
        preferred_element_type=F32,
    )


def kernel(
    rounds,
    sizes,
    rhs_ref,
    prec_ref,
    visc_ref,
    stiff_ref,
    cells_ref,
    live_ref,
    shared_ref,
    parents_ref,
    sol_ref,
    res_ref,
    ext_ref,
    x_ref,
    r_ref,
    search_ref,
    image_ref,
    pre_ref,
    where_ref,
    weight_ref,
    matrix_ref,
    node_ref,
    tail_ref,
    band_ref,
    place_ref,
    u_ref,
    tail_u_ref,
    hang_ref,
    piece_ref,
    acc_ref,
    step_ref,
    send_ref,
    recv_ref,
    red_ref,
    sum_ref,
    send_sem,
    recv_sem,
    rsend_sem,
    rrecv_sem,
):
    n_grp, n_cur = sizes
    devices = n_grp * n_cur
    my_grp = lax.axis_index("grp")
    my_cur = lax.axis_index("cur")
    me = my_grp * n_cur + my_cur

    def ring(offset):
        other = lax.rem(me + offset + devices, devices)
        return {"grp": other // n_cur, "cur": lax.rem(other, n_cur)}

    def my_place(r):
        axis, stride, size = rounds[r]
        mine = my_cur if axis == "cur" else my_grp
        return lax.rem(mine // stride, size)

    def partner(r, j):
        axis, stride, size = rounds[r]
        mine = my_cur if axis == "cur" else my_grp
        place = my_place(r)
        return {axis: mine + (lax.rem(place + j, size) - place) * stride}

    barrier = pltpu.get_barrier_semaphore()
    targets = [ring(-1), ring(1)]
    for r, (_, _, size) in enumerate(rounds):
        targets += [partner(r, j) for j in range(1, size)]
    for target in targets:
        pl.semaphore_signal(barrier, inc=1, device_id=target, device_id_type=MESH)

    has = [
        jnp.where(me > 0, 1.0, 0.0).astype(F32),
        jnp.where(me < devices - 1, 1.0, 0.0).astype(F32),
    ]

    def exchange(number):
        copies = []
        for side, offset in ((0, -1), (1, 1)):
            copies.append(
                pltpu.make_async_remote_copy(
                    src_ref=send_ref.at[number, side],
                    dst_ref=recv_ref.at[number, 1 - side],
                    send_sem=send_sem.at[number, side],
                    recv_sem=recv_sem.at[number, 1 - side],
                    device_id=ring(offset),
                    device_id_type=MESH,
                )
            )
        return copies

    def reduce_send(it, r):
        _, _, size = rounds[r]
        spot = my_place(r)
        red_ref[it, r, spot] = sum_ref[it, r]
        for j in range(1, size):
            pltpu.make_async_remote_copy(
                src_ref=sum_ref.at[it, r],
                dst_ref=red_ref.at[it, r, spot],
                send_sem=rsend_sem.at[it, r],
                recv_sem=rrecv_sem.at[it, r],
                device_id=partner(r, j),
                device_id_type=MESH,
            ).start()

    def reduce_wait(it, r):
        _, _, size = rounds[r]
        block = red_ref.at[it, r, pl.ds(0, size - 1)]
        pltpu.make_async_copy(block, block, rrecv_sem.at[it, r]).wait()
        total = red_ref[it, r, 0]
        for j in range(1, size):
            total = total + red_ref[it, r, j]
        return total

    def reduce_step(it, r):
        sum_ref[it, r] = reduce_wait(it, r - 1)
        reduce_send(it, r)

    def reduce_end(it):
        total = reduce_wait(it, len(rounds) - 1)
        norm = jnp.sum(total[0:1], 1, keepdims=True)
        bent = jnp.sum(total[4:5], 1, keepdims=True)
        step = jnp.broadcast_to(norm / bent, (8, 128))
        step_ref[0] = step
        step_ref[1] = step

    shared_index = jnp.concatenate(
        [shared_ref[j : j + 1, q * 128 : (q + 1) * 128] for j in range(2) for q in range(4)], 0
    )
    outgoing = gather_tile(
        [lambda row, c=c: rhs_ref[c, row : row + 1, :] for c in range(3)]
        + [lambda row: prec_ref[row : row + 1, :]],
        range(OWN_ROWS),
        shared_index,
    )
    for side in range(2):
        for c in range(3):
            send_ref[0, side, c, 0:4, :] = outgoing[c][side * 4 : side * 4 + 4]
            send_ref[0, side, c, 4:8, :] = outgoing[3][side * 4 : side * 4 + 4]
    pl.semaphore_wait(barrier, len(targets))
    for copy in exchange(0):
        copy.start()

    shared_band, shared_place = folded(
        jnp.concatenate([shared_ref[0:1, :], shared_ref[1:2, :]], 1)
    )
    count = (lax.broadcasted_iota(jnp.int32, (1, 1024), 1) + 1).astype(F32)
    where_ref[...] = halves(own_part(spread_dot(shared_band, shared_place, [count], False), 0))

    def moved(index):
        found = gather_tile([lambda row: where_ref[row : row + 1, :]], range(OWN_ROWS), index)[0]
        beyond = jnp.where(index >= 72 * 128, index + 1024, index)
        return jnp.where(found > 0.5, found.astype(jnp.int32) + (72 * 128 - 1), beyond)

    stays = where_ref[...] < 0.5
    pre_ref[0:OWN_ROWS, :] = jnp.where(stays, prec_ref[...], 0.0)
    pre_ref[SHARED, :] = outgoing[3]
    pre_ref[GHOSTS, :] = jnp.zeros((8, 128), F32)
    for c in range(3):
        r_ref[c, 0:OWN_ROWS, :] = jnp.where(stays, rhs_ref[c], 0.0)
        r_ref[c, SHARED, :] = outgoing[c]
        r_ref[c, GHOSTS, :] = jnp.zeros((8, 128), F32)
        search = pre_ref[...] * r_ref[c]
        search_ref[c] = search
        ext_ref[c, 0:80, :] = search
    x_ref[...] = jnp.zeros_like(x_ref)
    image_ref[...] = jnp.zeros_like(image_ref)
    u_ref[...] = jnp.zeros_like(u_ref)
    piece_ref[...] = jnp.zeros_like(piece_ref)
    step_ref[0] = jnp.zeros((8, 128), F32)
    step_ref[1] = jnp.full((8, 128), -1.0, F32)

    band_ref[24:32, :] = jnp.zeros((8, 1024), jnp.int32)
    place_ref[24:32, :] = jnp.zeros((8, 1024), jnp.int32)
    parent_rows = [parents_ref[p : p + 1, q * 128 : (q + 1) * 128] for p in range(3) for q in range(2)]
    parent_index = moved(jnp.concatenate(parent_rows + parent_rows[:2], 0))
    parent_band, parent_place = folded(as_row(parent_index[0:6]))
    for k in range(24, 27):
        index = moved(
            jnp.concatenate([cells_ref[k : k + 1, s * 128 : s * 128 + 128] for s in range(8)], 0)
        )
        tail_ref[k - 24] = index
        band, place = folded(index)
        band_ref[k : k + 1, :] = as_row(band)
        place_ref[k : k + 1, :] = as_row(place)

    def columns_of(chunk):
        if isinstance(chunk, int):
            return pl.ds(chunk * 128, 128)
        return pl.ds(pl.multiple_of(chunk * 128, 128), 128)

    def move_chunk(chunk, _):
        for top in range(0, 24, 8):
            index = moved(cells_ref[top : top + 8, columns_of(chunk)])
            node_ref[top : top + 8, columns_of(chunk)] = index
            band, place = folded(index)
            band_ref[top : top + 8, columns_of(chunk)] = band
            place_ref[top : top + 8, columns_of(chunk)] = place
        return 0

    lax.fori_loop(0, CHUNKS, move_chunk, 0)
    slot = lax.broadcasted_iota(jnp.int32, (1, 1024), 1)
    weight_ref[...] = jnp.where(slot < live_ref[0], visc_ref[...], 0.0)
    at = lax.broadcasted_iota(jnp.int32, (96, 81), 0)
    want = jnp.where((at & 31) < 27, (at >> 5) * 27 + (at & 31), -1)
    pick = jnp.where(want == lax.broadcasted_iota(jnp.int32, (96, 81), 1), 1.0, 0.0).astype(BF16)

    def padded(part):
        rows = lax.dot_general(pick, part, (((1,), (1,)), ((), ())), preferred_element_type=F32)
        return lax.dot_general(
            rows.astype(BF16), pick, (((1,), (1,)), ((), ())), preferred_element_type=F32
        ).astype(BF16)

    stiff = stiff_ref[...]
    stiff_high = stiff.astype(BF16)
    matrix_ref[0] = padded(stiff_high)
    matrix_ref[1] = padded((stiff - stiff_high.astype(F32)).astype(BF16))

    fields = [lambda row, c=c: ext_ref[c, row : row + 1, :] for c in range(3)]
    early = range(OWN_ROWS)
    late = range(OWN_ROWS, EXT_ROWS)

    def gather(chunk, rows, go_on):
        for top in range(0, 24, 8):
            start = [u_ref[chunk, c, top : top + 8, :] for c in range(3)] if go_on else None
            got = gather_tile(fields, rows, node_ref[top : top + 8, columns_of(chunk)], start)
            for c in range(3):
                u_ref[chunk, c, top : top + 8, :] = got[c]

    def element(chunk):
        u = u_ref[chunk].reshape(96, 128)
        u_high = u.astype(BF16)
        u_low = (u - u_high.astype(F32)).astype(BF16)
        high, low = matrix_ref[0], matrix_ref[1]
        t = (
            jnp.dot(high, u_high, preferred_element_type=F32)
            + jnp.dot(high, u_low, preferred_element_type=F32)
            + jnp.dot(low, u_high, preferred_element_type=F32)
        ) * weight_ref[0:1, columns_of(chunk)]
        t_high = t.astype(BF16).astype(F32)
        t_low = t - t_high
        for c in range(3):
            own = slice(c * 32, c * 32 + 32)
            piece_ref[pl.ds(2 * c, 32, stride=8), :] = t_high[own]
            piece_ref[pl.ds(2 * c + 1, 32, stride=8), :] = t_low[own]

    def scatter(chunk):
        acc_ref[...] += chunk_dot(band_ref, place_ref, piece_ref, columns_of(chunk))

    def near_sums(number, c):
        return jnp.concatenate(
            [recv_ref[number, side, c, 0:4, :] for side in range(2)]
            + [recv_ref[number, side, c, 4:8, :] * has[side] for side in range(2)],
            0,
        )

    def finish_near(number):
        turn = step_ref[1, 0:1, :]
        for c in range(3):
            image = image_ref[c, NEAR, :] - turn * near_sums(number, c)
            image_ref[c, NEAR, :] = image
            ext_ref[c, NEAR, :] = pre_ref[NEAR, :] * image

    def iteration(it, _):
        for c, got in enumerate(gather_tile(fields, early, parent_index)):
            hang_ref[c] = got
        for k in range(3):
            for c, got in enumerate(gather_tile(fields, early, tail_ref[k])):
                tail_u_ref[k, c] = got

        def early_step(chunk, _):
            gather(chunk, early, False)
            return 0

        lax.fori_loop(0, EARLY, early_step, 0)

        @pl.when(it > 0)
        def _():
            for r in range(1, len(rounds)):
                reduce_step(it - 1, r)

        for copy in exchange(it):
            copy.wait()

        @pl.when(it == 0)
        def _():
            for side in range(2):
                own = slice(64 + side * 4, 68 + side * 4)
                scale = recv_ref[0, side, 0, 4:8, :] * has[side]
                pre_ref[own, :] = scale
                for c in range(3):
                    ghost = recv_ref[0, side, c, 0:4, :]
                    r_ref[c, own, :] = ghost
                    ext_ref[c, own, :] = scale * ghost

        @pl.when(it > 0)
        def _():
            finish_near(it)

        found = gather_tile(
            fields, range(OWN_ROWS, 80), parent_index, [hang_ref[c] for c in range(3)]
        )
        for c in range(3):
            ext_ref[c, 80:82, :] = (
                0.375 * found[c][0:2] + 0.75 * found[c][2:4] - 0.125 * found[c][4:6]
            )
        acc_ref[...] = jnp.zeros_like(acc_ref)
        for k in range(3):
            got = gather_tile(fields, late, tail_ref[k], [tail_u_ref[k, c] for c in range(3)])
            for c in range(3):
                for s in range(CHUNKS):
                    u_ref[s, c, 24 + k : 25 + k, :] = got[c][s : s + 1]
        gather(0, late, True)

        def late_step(chunk, _):
            element(chunk)
            gather(chunk + 1, late, True)
            scatter(chunk)
            return 0

        def whole_step(chunk, _):
            element(chunk)
            gather(chunk + 1, range(EXT_ROWS), False)
            scatter(chunk)
            return 0

        lax.fori_loop(0, EARLY - 1, late_step, 0)
        if EARLY < CHUNKS:
            lax.fori_loop(EARLY - 1, CHUNKS - 1, whole_step, 0)
        element(CHUNKS - 1)
        scatter(CHUNKS - 1)

        hanging = [hang_part(acc_ref, c) for c in range(3)]
        fold = spread_dot(
            parent_band,
            parent_place,
            [jnp.concatenate([0.375 * h, 0.75 * h, -0.125 * h], 1) for h in hanging],
        )
        number = it + 1
        near = []
        for c in range(3):
            near.append(near_rows(extra_part(acc_ref, c) + extra_part(fold, c)))
            for side in range(2):
                send_ref[number, side, c, 0:4, :] = near[c][8 + side * 4 : 12 + side * 4]
                send_ref[number, side, c, 4:8, :] = near[c][side * 4 : side * 4 + 4]
        for copy in exchange(number):
            copy.start()

        @pl.when(it > 0)
        def _():
            reduce_end(it - 1)

        step = step_ref[0, 0:1, :]
        turn = step_ref[1, 0:1, :]
        norm = jnp.zeros((1, 128), F32)
        bent = jnp.zeros((1, 128), F32)
        for c in range(3):
            x_ref[c] = x_ref[c] + step * search_ref[c]
            residual = r_ref[c] - step * image_ref[c]
            r_ref[c] = residual
            search = pre_ref[...] * residual
            search_ref[c] = search
            part = jnp.concatenate([halves(own_part(acc_ref, c) + own_part(fold, c)), near[c]], 0)
            change = turn * part
            image = image_ref[c] - change
            image_ref[c] = image
            ext_ref[c, 0:OWN_ROWS, :] = pre_ref[0:OWN_ROWS, :] * image[0:OWN_ROWS]
            for own in (slice(0, OWN_ROWS), SHARED):
                norm = norm + jnp.sum(residual[own] * search[own], 0, keepdims=True)
                bent = bent + jnp.sum(search[own] * image[own], 0, keepdims=True)
            bent = bent - jnp.sum(search[GHOSTS] * change[GHOSTS], 0, keepdims=True)
        sum_ref[it, 0] = jnp.concatenate(
            [jnp.broadcast_to(norm, (4, 128)), jnp.broadcast_to(bent, (4, 128))], 0
        )
        reduce_send(it, 0)
        return 0

    lax.fori_loop(0, ITERS, iteration, 0)
    for copy in exchange(ITERS):
        copy.wait()
    finish_near(ITERS)
    last = ITERS - 1
    home = []
    for values_ref in (x_ref, search_ref, r_ref, image_ref):
        home.append(
            spread_dot(
                shared_band, shared_place, [as_row(values_ref[c, SHARED, :]) for c in range(3)], False
            )
        )
    for r in range(1, len(rounds)):
        reduce_step(last, r)
    reduce_end(last)
    step = step_ref[0, 0:1, :]

    def whole(values_ref, spread, c):
        return values_ref[c, 0:OWN_ROWS, :] + halves(own_part(spread, c))

    for c in range(3):
        sol_ref[c] = whole(x_ref, home[0], c) + step * whole(search_ref, home[1], c)
        res_ref[c] = whole(r_ref, home[2], c) - step * whole(image_ref, home[3], c)
    for it in range(ITERS):
        for r, (_, _, size) in enumerate(rounds):
            block = red_ref.at[it, r, pl.ds(0, size - 1)]
            pltpu.make_async_copy(block, block, rsend_sem.at[it, r]).wait()


def make_local(n_grp, n_cur):
    rounds = []
    rest, stride = n_cur, 1
    while rest > 1:
        size = min(32, rest)
        rounds.append(("cur", stride, size))
        stride, rest = stride * size, rest // size
    if n_grp > 1:
        rounds.append(("grp", 1, n_grp))
    widest = max(size for _, _, size in rounds)

    def local(
        right_side, precond, viscosity, stiffness, element_nodes, live, shared, parents
    ):
        vmem = pl.BlockSpec(memory_space=pltpu.VMEM)
        smem = pl.BlockSpec(memory_space=pltpu.SMEM)
        shape = jax.ShapeDtypeStruct((3, OWN_ROWS, 128), F32)
        call = pl.pallas_call(
            functools.partial(kernel, tuple(rounds), (n_grp, n_cur)),
            out_shape=(shape, shape),
            in_specs=[vmem, vmem, vmem, vmem, vmem, smem, vmem, vmem],
            out_specs=(vmem, vmem),
            scratch_shapes=[
                pltpu.VMEM((3, 88, 128), F32),
                pltpu.VMEM((3, 80, 128), F32),
                pltpu.VMEM((3, 80, 128), F32),
                pltpu.VMEM((3, 80, 128), F32),
                pltpu.VMEM((3, 80, 128), F32),
                pltpu.VMEM((80, 128), F32),
                pltpu.VMEM((OWN_ROWS, 128), F32),
                pltpu.VMEM((1, 1024), F32),
                pltpu.VMEM((2, 96, 96), BF16),
                pltpu.VMEM((24, 1024), jnp.int32),
                pltpu.VMEM((3, 8, 128), jnp.int32),
                pltpu.VMEM((32, 1024), jnp.int32),
                pltpu.VMEM((32, 1024), jnp.int32),
                pltpu.VMEM((CHUNKS, 3, 32, 128), F32),
                pltpu.VMEM((3, 3, 8, 128), F32),
                pltpu.VMEM((3, 8, 128), F32),
                pltpu.VMEM((256, 128), F32),
                pltpu.VMEM((256, 256), F32),
                pltpu.VMEM((2, 8, 128), F32),
                pltpu.VMEM((ITERS + 1, 2, 3, 8, 128), F32),
                pltpu.VMEM((ITERS + 1, 2, 3, 8, 128), F32),
                pltpu.VMEM((ITERS, len(rounds), widest, 8, 128), F32),
                pltpu.VMEM((ITERS, len(rounds), 8, 128), F32),
                pltpu.SemaphoreType.DMA((ITERS + 1, 2)),
                pltpu.SemaphoreType.DMA((ITERS + 1, 2)),
                pltpu.SemaphoreType.DMA((ITERS, len(rounds))),
                pltpu.SemaphoreType.DMA((ITERS, len(rounds))),
            ],
            compiler_params=pltpu.CompilerParams(
                collective_id=0, has_side_effects=True, vmem_limit_bytes=48 * 1024 * 1024
            ),
            name="descent",
        )
        sol, res = call(
            right_side.reshape(3, OWN_ROWS, 128),
            precond.reshape(OWN_ROWS, 128),
            viscosity.reshape(1, 1024),
            stiffness,
            element_nodes,
            live,
            shared,
            parents,
        )
        return sol.reshape(3, OWN_ROWS * 128), res.reshape(3, OWN_ROWS * 128)

    return local


def solution(mesh):
    both = ("grp", "cur")
    in_specs = (
        P(None, both),
        P(both),
        P(both),
        P(),
        P(None, both),
        P(both),
        P(None, both),
        P(None, both),
    )
    out_specs = (P(None, both), P(None, both))
    return jax.shard_map(
        make_local(mesh.shape["grp"], mesh.shape["cur"]),
        mesh=mesh,
        in_specs=in_specs,
        out_specs=out_specs,
        check_vma=False,
    )
```

```python
import functools

import jax
import jax.numpy as jnp
from jax import lax
from jax.experimental import pallas as pl
from jax.experimental.pallas import tpu as pltpu
from jax.sharding import PartitionSpec as P

ITERS = 3
F32 = jnp.float32
BF16 = jnp.bfloat16
MESH = pl.DeviceIdType.MESH
OWN_ROWS = 64
NEAR = slice(64, 80)
GHOSTS = slice(64, 72)
SHARED = slice(72, 80)
EXT_ROWS = 82
EARLY = 3
CHUNKS = 8
NODES = 28


def take(src, lanes):
    return jnp.take_along_axis(src, lanes, axis=1, mode="promise_in_bounds")


def gather_tile(fields, rows, index, found=None):
    lanes = index & 127
    own = index >> 7
    found = list(found) if found else [jnp.zeros((8, 128), F32) for _ in fields]
    for row in rows:
        hit = own == row
        for i, field in enumerate(fields):
            line = jnp.broadcast_to(field(row), (8, 128))
            found[i] = jnp.where(hit, take(line, lanes), found[i])
    return found


def folded(index):
    row = index >> 7
    lane = index & 127
    own = row < 64
    hang = row >= 80
    near = 32 + (row & 3) + jnp.where(row >= 72, 4, 0)
    band = jnp.where(own, row & 31, jnp.where(hang, 40, near))
    half = jnp.where(own, row >> 5, jnp.where(hang, row & 1, (row >> 2) & 1))
    return band, half * 128 + lane


def pieces(row):
    high = row.astype(BF16)
    low = (row - high.astype(F32)).astype(BF16)
    return high, low


def spread_dot(band, place, values, extra=True):
    n = band.shape[1]
    band16 = band.astype(jnp.int16)
    place16 = place.astype(jnp.int16)
    zero = jnp.zeros((16, n), BF16)
    one = jnp.ones((256, n), BF16)
    hot = jnp.where(
        lax.broadcasted_iota(jnp.int16, (256, n), 0) == place16, one, jnp.zeros((256, n), BF16)
    )
    line = lax.broadcasted_iota(jnp.int16, (16, n), 0)
    hit0 = line == band16
    hit1 = (line + jnp.int16(16)) == band16
    parts = []
    tails = []
    if extra:
        first = line < jnp.int16(8)
        hit2 = jnp.where(first, line, line - jnp.int16(8)) == (band16 - jnp.int16(32))
    for value in values:
        high, low = pieces(value)
        high = jnp.broadcast_to(high, (16, n))
        low = jnp.broadcast_to(low, (16, n))
        for piece in (high, low):
            parts.append(jnp.where(hit0, piece, zero))
            parts.append(jnp.where(hit1, piece, zero))
        if extra:
            tails.append(jnp.where(hit2, jnp.where(first, high, low), zero))
    left = jnp.concatenate(parts + tails, 0)
    return lax.dot_general(left, hot, (((1,), (1,)), ((), ())), preferred_element_type=F32)


def own_part(total, c):
    return total[c * 64 : c * 64 + 32] + total[c * 64 + 32 : c * 64 + 64]


def extra_part(total, c):
    return total[192 + c * 16 : 200 + c * 16] + total[200 + c * 16 : 208 + c * 16]


def hang_part(total, c):
    return total[240 + 2 * c : 241 + 2 * c] + total[241 + 2 * c : 242 + 2 * c]


def as_row(block):
    return jnp.concatenate([block[i : i + 1] for i in range(block.shape[0])], 1)


def halves(wide):
    return jnp.concatenate([wide[:, 0:128], wide[:, 128:256]], 0)


def near_rows(wide):
    return jnp.concatenate(
        [wide[0:4, 0:128], wide[0:4, 128:256], wide[4:8, 0:128], wide[4:8, 128:256]], 0
    )


def chunk_dot(band_ref, place_ref, piece_ref, columns):
    zero = jnp.zeros((16, 128), BF16)
    one = jnp.ones((16, 128), BF16)
    line = lax.broadcasted_iota(jnp.int16, (16, 128), 0)
    lines = [line + jnp.int16(16 * i) for i in range(16)]
    first = line < jnp.int16(8)
    beyond = jnp.where(first, line, line - jnp.int16(8)) + jnp.int16(32)
    hots, lefts = [], []
    for k in range(NODES):
        band = jnp.broadcast_to(band_ref[k : k + 1, columns], (16, 128)).astype(jnp.int16)
        place = jnp.broadcast_to(place_ref[k : k + 1, columns], (16, 128)).astype(jnp.int16)
        hots.append(jnp.concatenate([jnp.where(at == place, one, zero) for at in lines], 0))
        hits = [lines[0] == band, lines[1] == band]
        hit_beyond = beyond == band
        parts, tails = [], []
        for c in range(3):
            row = k * 8 + c * 2
            pair = [
                jnp.broadcast_to(piece_ref[row + p : row + p + 1, :], (16, 128)).astype(BF16)
                for p in range(2)
            ]
            parts += [jnp.where(hit, piece, zero) for piece in pair for hit in hits]
            tails.append(jnp.where(hit_beyond, jnp.where(first, pair[0], pair[1]), zero))
        block = piece_ref[k * 8 : k * 8 + 8, :]
        block = jnp.concatenate([block, jnp.zeros((8, 128), F32)], 0).astype(BF16)
        tails.append(jnp.where(band == jnp.int16(40), block, zero))
        lefts.append(jnp.concatenate(parts + tails, 0))
    return lax.dot_general(
        jnp.concatenate(lefts, 1),
        jnp.concatenate(hots, 1),
        (((1,), (1,)), ((), ())),
        preferred_element_type=F32,
    )


def kernel(
    rounds,
    sizes,
    rhs_ref,
    prec_ref,
    visc_ref,
    stiff_ref,
    cells_ref,
    live_ref,
    shared_ref,
    parents_ref,
    sol_ref,
    res_ref,
    ext_ref,
    x_ref,
    r_ref,
    search_ref,
    image_ref,
    pre_ref,
    where_ref,
    weight_ref,
    matrix_ref,
    node_ref,
    tail_ref,
    band_ref,
    place_ref,
    u_ref,
    tail_u_ref,
    hang_ref,
    piece_ref,
    acc_ref,
    step_ref,
    send_ref,
    recv_ref,
    red_ref,
    sum_ref,
    send_sem,
    recv_sem,
    rsend_sem,
    rrecv_sem,
):
    n_grp, n_cur = sizes
    devices = n_grp * n_cur
    my_grp = lax.axis_index("grp")
    my_cur = lax.axis_index("cur")
    me = my_grp * n_cur + my_cur

    def ring(offset):
        other = lax.rem(me + offset + devices, devices)
        return {"grp": other // n_cur, "cur": lax.rem(other, n_cur)}

    def my_place(r):
        axis, stride, size = rounds[r]
        mine = my_cur if axis == "cur" else my_grp
        return lax.rem(mine // stride, size)

    def partner(r, j):
        axis, stride, size = rounds[r]
        mine = my_cur if axis == "cur" else my_grp
        place = my_place(r)
        return {axis: mine + (lax.rem(place + j, size) - place) * stride}

    barrier = pltpu.get_barrier_semaphore()
    targets = [ring(-1), ring(1)]
    for r, (_, _, size) in enumerate(rounds):
        targets += [partner(r, j) for j in range(1, size)]
    for target in targets:
        pl.semaphore_signal(barrier, inc=1, device_id=target, device_id_type=MESH)

    has = [
        jnp.where(me > 0, 1.0, 0.0).astype(F32),
        jnp.where(me < devices - 1, 1.0, 0.0).astype(F32),
    ]

    def exchange(number):
        copies = []
        for side, offset in ((0, -1), (1, 1)):
            copies.append(
                pltpu.make_async_remote_copy(
                    src_ref=send_ref.at[number, side],
                    dst_ref=recv_ref.at[number, 1 - side],
                    send_sem=send_sem.at[number, side],
                    recv_sem=recv_sem.at[number, 1 - side],
                    device_id=ring(offset),
                    device_id_type=MESH,
                )
            )
        return copies

    def reduce_send(it, r):
        _, _, size = rounds[r]
        spot = my_place(r)
        red_ref[it, r, spot] = sum_ref[it, r]
        for j in range(1, size):
            pltpu.make_async_remote_copy(
                src_ref=sum_ref.at[it, r],
                dst_ref=red_ref.at[it, r, spot],
                send_sem=rsend_sem.at[it, r],
                recv_sem=rrecv_sem.at[it, r],
                device_id=partner(r, j),
                device_id_type=MESH,
            ).start()

    def reduce_wait(it, r):
        _, _, size = rounds[r]
        block = red_ref.at[it, r, pl.ds(0, size - 1)]
        pltpu.make_async_copy(block, block, rrecv_sem.at[it, r]).wait()
        total = red_ref[it, r, 0]
        for j in range(1, size):
            total = total + red_ref[it, r, j]
        return total

    def reduce_step(it, r):
        sum_ref[it, r] = reduce_wait(it, r - 1)
        reduce_send(it, r)

    def reduce_end(it):
        total = reduce_wait(it, len(rounds) - 1)
        norm = jnp.sum(total[0:1], 1, keepdims=True)
        bent = jnp.sum(total[4:5], 1, keepdims=True)
        step = jnp.broadcast_to(norm / bent, (8, 128))
        step_ref[0] = step
        step_ref[1] = step

    shared_index = jnp.concatenate(
        [shared_ref[j : j + 1, q * 128 : (q + 1) * 128] for j in range(2) for q in range(4)], 0
    )
    outgoing = gather_tile(
        [lambda row, c=c: rhs_ref[c, row : row + 1, :] for c in range(3)]
        + [lambda row: prec_ref[row : row + 1, :]],
        range(OWN_ROWS),
        shared_index,
    )
    for side in range(2):
        for c in range(3):
            send_ref[0, side, c, 0:4, :] = outgoing[c][side * 4 : side * 4 + 4]
            send_ref[0, side, c, 4:8, :] = outgoing[3][side * 4 : side * 4 + 4]
    pl.semaphore_wait(barrier, len(targets))
    for copy in exchange(0):
        copy.start()

    shared_band, shared_place = folded(
        jnp.concatenate([shared_ref[0:1, :], shared_ref[1:2, :]], 1)
    )
    count = (lax.broadcasted_iota(jnp.int32, (1, 1024), 1) + 1).astype(F32)
    where_ref[...] = halves(own_part(spread_dot(shared_band, shared_place, [count], False), 0))

    def moved(index):
        found = gather_tile([lambda row: where_ref[row : row + 1, :]], range(OWN_ROWS), index)[0]
        beyond = jnp.where(index >= 72 * 128, index + 1024, index)
        return jnp.where(found > 0.5, found.astype(jnp.int32) + (72 * 128 - 1), beyond)

    stays = where_ref[...] < 0.5
    pre_ref[0:OWN_ROWS, :] = jnp.where(stays, prec_ref[...], 0.0)
    pre_ref[SHARED, :] = outgoing[3]
    pre_ref[GHOSTS, :] = jnp.zeros((8, 128), F32)
    for c in range(3):
        r_ref[c, 0:OWN_ROWS, :] = jnp.where(stays, rhs_ref[c], 0.0)
        r_ref[c, SHARED, :] = outgoing[c]
        r_ref[c, GHOSTS, :] = jnp.zeros((8, 128), F32)
        search = pre_ref[...] * r_ref[c]
        search_ref[c] = search
        ext_ref[c, 0:80, :] = search
    x_ref[...] = jnp.zeros_like(x_ref)
    image_ref[...] = jnp.zeros_like(image_ref)
    u_ref[...] = jnp.zeros_like(u_ref)
    piece_ref[...] = jnp.zeros_like(piece_ref)
    step_ref[0] = jnp.zeros((8, 128), F32)
    step_ref[1] = jnp.full((8, 128), -1.0, F32)

    band_ref[24:32, :] = jnp.zeros((8, 1024), jnp.int32)
    place_ref[24:32, :] = jnp.zeros((8, 1024), jnp.int32)
    parent_rows = [parents_ref[p : p + 1, q * 128 : (q + 1) * 128] for p in range(3) for q in range(2)]
    parent_index = moved(jnp.concatenate(parent_rows + parent_rows[:2], 0))
    parent_band, parent_place = folded(as_row(parent_index[0:6]))
    for k in range(24, 27):
        index = moved(
            jnp.concatenate([cells_ref[k : k + 1, s * 128 : s * 128 + 128] for s in range(8)], 0)
        )
        tail_ref[k - 24] = index
        band, place = folded(index)
        band_ref[k : k + 1, :] = as_row(band)
        place_ref[k : k + 1, :] = as_row(place)

    def columns_of(chunk):
        if isinstance(chunk, int):
            return pl.ds(chunk * 128, 128)
        return pl.ds(pl.multiple_of(chunk * 128, 128), 128)

    def move_chunk(chunk, _):
        for top in range(0, 24, 8):
            index = moved(cells_ref[top : top + 8, columns_of(chunk)])
            node_ref[top : top + 8, columns_of(chunk)] = index
            band, place = folded(index)
            band_ref[top : top + 8, columns_of(chunk)] = band
            place_ref[top : top + 8, columns_of(chunk)] = place
        return 0

    lax.fori_loop(0, CHUNKS, move_chunk, 0)
    slot = lax.broadcasted_iota(jnp.int32, (1, 1024), 1)
    weight_ref[...] = jnp.where(slot < live_ref[0], visc_ref[...], 0.0)
    at = lax.broadcasted_iota(jnp.int32, (96, 81), 0)
    want = jnp.where((at & 31) < 27, (at >> 5) * 27 + (at & 31), -1)
    pick = jnp.where(want == lax.broadcasted_iota(jnp.int32, (96, 81), 1), 1.0, 0.0).astype(BF16)

    def padded(part):
        rows = lax.dot_general(pick, part, (((1,), (1,)), ((), ())), preferred_element_type=F32)
        return lax.dot_general(
            rows.astype(BF16), pick, (((1,), (1,)), ((), ())), preferred_element_type=F32
        ).astype(BF16)

    stiff = stiff_ref[...]
    stiff_high = stiff.astype(BF16)
    matrix_ref[0] = padded(stiff_high)
    matrix_ref[1] = padded((stiff - stiff_high.astype(F32)).astype(BF16))

    fields = [lambda row, c=c: ext_ref[c, row : row + 1, :] for c in range(3)]
    early = range(OWN_ROWS)
    late = range(OWN_ROWS, EXT_ROWS)

    def gather(chunk, rows, go_on):
        for top in range(0, 24, 8):
            start = [u_ref[chunk, c, top : top + 8, :] for c in range(3)] if go_on else None
            got = gather_tile(fields, rows, node_ref[top : top + 8, columns_of(chunk)], start)
            for c in range(3):
                u_ref[chunk, c, top : top + 8, :] = got[c]

    def element(chunk):
        u = u_ref[chunk].reshape(96, 128)
        u_high = u.astype(BF16)
        u_low = (u - u_high.astype(F32)).astype(BF16)
        high, low = matrix_ref[0], matrix_ref[1]
        t = (
            jnp.dot(high, u_high, preferred_element_type=F32)
            + jnp.dot(high, u_low, preferred_element_type=F32)
            + jnp.dot(low, u_high, preferred_element_type=F32)
        ) * weight_ref[0:1, columns_of(chunk)]
        t_high = t.astype(BF16).astype(F32)
        t_low = t - t_high
        for c in range(3):
            own = slice(c * 32, c * 32 + 32)
            piece_ref[pl.ds(2 * c, 32, stride=8), :] = t_high[own]
            piece_ref[pl.ds(2 * c + 1, 32, stride=8), :] = t_low[own]

    def scatter(chunk):
        acc_ref[...] += chunk_dot(band_ref, place_ref, piece_ref, columns_of(chunk))

    def near_sums(number, c):
        return jnp.concatenate(
            [recv_ref[number, side, c, 0:4, :] for side in range(2)]
            + [recv_ref[number, side, c, 4:8, :] * has[side] for side in range(2)],
            0,
        )

    def finish_near(number):
        turn = step_ref[1, 0:1, :]
        for c in range(3):
            image = image_ref[c, NEAR, :] - turn * near_sums(number, c)
            image_ref[c, NEAR, :] = image
            ext_ref[c, NEAR, :] = pre_ref[NEAR, :] * image

    def iteration(it, _):
        for c, got in enumerate(gather_tile(fields, early, parent_index)):
            hang_ref[c] = got
        for k in range(3):
            for c, got in enumerate(gather_tile(fields, early, tail_ref[k])):
                tail_u_ref[k, c] = got

        def early_step(chunk, _):
            gather(chunk, early, False)
            return 0

        lax.fori_loop(0, EARLY, early_step, 0)

        for copy in exchange(it):
            copy.wait()

        @pl.when(it == 0)
        def _():
            for side in range(2):
                own = slice(64 + side * 4, 68 + side * 4)
                scale = recv_ref[0, side, 0, 4:8, :] * has[side]
                pre_ref[own, :] = scale
                for c in range(3):
                    ghost = recv_ref[0, side, c, 0:4, :]
                    r_ref[c, own, :] = ghost
                    ext_ref[c, own, :] = scale * ghost

        @pl.when(it > 0)
        def _():
            finish_near(it)

        found = gather_tile(
            fields, range(OWN_ROWS, 80), parent_index, [hang_ref[c] for c in range(3)]
        )
        for c in range(3):
            ext_ref[c, 80:82, :] = (
                0.375 * found[c][0:2] + 0.75 * found[c][2:4] - 0.125 * found[c][4:6]
            )
        acc_ref[...] = jnp.zeros_like(acc_ref)
        for k in range(3):
            got = gather_tile(fields, late, tail_ref[k], [tail_u_ref[k, c] for c in range(3)])
            for c in range(3):
                for s in range(CHUNKS):
                    u_ref[s, c, 24 + k : 25 + k, :] = got[c][s : s + 1]
        gather(0, late, True)

        @pl.when(it > 0)
        def _():
            for r in range(1, len(rounds)):
                reduce_step(it - 1, r)

        def late_step(chunk, _):
            element(chunk)
            gather(chunk + 1, late, True)
            scatter(chunk)
            return 0

        def whole_step(chunk, _):
            element(chunk)
            gather(chunk + 1, range(EXT_ROWS), False)
            scatter(chunk)
            return 0

        lax.fori_loop(0, EARLY - 1, late_step, 0)
        if EARLY < CHUNKS:
            lax.fori_loop(EARLY - 1, CHUNKS - 1, whole_step, 0)
        element(CHUNKS - 1)
        scatter(CHUNKS - 1)

        hanging = [hang_part(acc_ref, c) for c in range(3)]
        fold = spread_dot(
            parent_band,
            parent_place,
            [jnp.concatenate([0.375 * h, 0.75 * h, -0.125 * h], 1) for h in hanging],
        )
        number = it + 1
        near = []
        for c in range(3):
            near.append(near_rows(extra_part(acc_ref, c) + extra_part(fold, c)))
            for side in range(2):
                send_ref[number, side, c, 0:4, :] = near[c][8 + side * 4 : 12 + side * 4]
                send_ref[number, side, c, 4:8, :] = near[c][side * 4 : side * 4 + 4]
        for copy in exchange(number):
            copy.start()

        @pl.when(it > 0)
        def _():
            reduce_end(it - 1)

        step = step_ref[0, 0:1, :]
        turn = step_ref[1, 0:1, :]
        norm = jnp.zeros((1, 128), F32)
        bent = jnp.zeros((1, 128), F32)
        for c in range(3):
            x_ref[c] = x_ref[c] + step * search_ref[c]
            residual = r_ref[c] - step * image_ref[c]
            r_ref[c] = residual
            search = pre_ref[...] * residual
            search_ref[c] = search
            part = jnp.concatenate([halves(own_part(acc_ref, c) + own_part(fold, c)), near[c]], 0)
            change = turn * part
            image = image_ref[c] - change
            image_ref[c] = image
            ext_ref[c, 0:OWN_ROWS, :] = pre_ref[0:OWN_ROWS, :] * image[0:OWN_ROWS]
            for own in (slice(0, OWN_ROWS), SHARED):
                norm = norm + jnp.sum(residual[own] * search[own], 0, keepdims=True)
                bent = bent + jnp.sum(search[own] * image[own], 0, keepdims=True)
            bent = bent - jnp.sum(search[GHOSTS] * change[GHOSTS], 0, keepdims=True)
        sum_ref[it, 0] = jnp.concatenate(
            [jnp.broadcast_to(norm, (4, 128)), jnp.broadcast_to(bent, (4, 128))], 0
        )
        reduce_send(it, 0)
        return 0

    lax.fori_loop(0, ITERS, iteration, 0)
    for copy in exchange(ITERS):
        copy.wait()
    finish_near(ITERS)
    last = ITERS - 1
    home = []
    for values_ref in (x_ref, search_ref, r_ref, image_ref):
        home.append(
            spread_dot(
                shared_band, shared_place, [as_row(values_ref[c, SHARED, :]) for c in range(3)], False
            )
        )
    for r in range(1, len(rounds)):
        reduce_step(last, r)
    reduce_end(last)
    step = step_ref[0, 0:1, :]

    def whole(values_ref, spread, c):
        return values_ref[c, 0:OWN_ROWS, :] + halves(own_part(spread, c))

    for c in range(3):
        sol_ref[c] = whole(x_ref, home[0], c) + step * whole(search_ref, home[1], c)
        res_ref[c] = whole(r_ref, home[2], c) - step * whole(image_ref, home[3], c)
    for it in range(ITERS):
        for r, (_, _, size) in enumerate(rounds):
            block = red_ref.at[it, r, pl.ds(0, size - 1)]
            pltpu.make_async_copy(block, block, rsend_sem.at[it, r]).wait()


def make_local(n_grp, n_cur):
    rounds = []
    rest, stride = n_cur, 1
    while rest > 1:
        size = min(32, rest)
        rounds.append(("cur", stride, size))
        stride, rest = stride * size, rest // size
    if n_grp > 1:
        rounds.append(("grp", 1, n_grp))
    widest = max(size for _, _, size in rounds)

    def local(
        right_side, precond, viscosity, stiffness, element_nodes, live, shared, parents
    ):
        vmem = pl.BlockSpec(memory_space=pltpu.VMEM)
        smem = pl.BlockSpec(memory_space=pltpu.SMEM)
        shape = jax.ShapeDtypeStruct((3, OWN_ROWS, 128), F32)
        call = pl.pallas_call(
            functools.partial(kernel, tuple(rounds), (n_grp, n_cur)),
            out_shape=(shape, shape),
            in_specs=[vmem, vmem, vmem, vmem, vmem, smem, vmem, vmem],
            out_specs=(vmem, vmem),
            scratch_shapes=[
                pltpu.VMEM((3, 88, 128), F32),
                pltpu.VMEM((3, 80, 128), F32),
                pltpu.VMEM((3, 80, 128), F32),
                pltpu.VMEM((3, 80, 128), F32),
                pltpu.VMEM((3, 80, 128), F32),
                pltpu.VMEM((80, 128), F32),
                pltpu.VMEM((OWN_ROWS, 128), F32),
                pltpu.VMEM((1, 1024), F32),
                pltpu.VMEM((2, 96, 96), BF16),
                pltpu.VMEM((24, 1024), jnp.int32),
                pltpu.VMEM((3, 8, 128), jnp.int32),
                pltpu.VMEM((32, 1024), jnp.int32),
                pltpu.VMEM((32, 1024), jnp.int32),
                pltpu.VMEM((CHUNKS, 3, 32, 128), F32),
                pltpu.VMEM((3, 3, 8, 128), F32),
                pltpu.VMEM((3, 8, 128), F32),
                pltpu.VMEM((256, 128), F32),
                pltpu.VMEM((256, 256), F32),
                pltpu.VMEM((2, 8, 128), F32),
                pltpu.VMEM((ITERS + 1, 2, 3, 8, 128), F32),
                pltpu.VMEM((ITERS + 1, 2, 3, 8, 128), F32),
                pltpu.VMEM((ITERS, len(rounds), widest, 8, 128), F32),
                pltpu.VMEM((ITERS, len(rounds), 8, 128), F32),
                pltpu.SemaphoreType.DMA((ITERS + 1, 2)),
                pltpu.SemaphoreType.DMA((ITERS + 1, 2)),
                pltpu.SemaphoreType.DMA((ITERS, len(rounds))),
                pltpu.SemaphoreType.DMA((ITERS, len(rounds))),
            ],
            compiler_params=pltpu.CompilerParams(
                collective_id=0, has_side_effects=True, vmem_limit_bytes=48 * 1024 * 1024
            ),
            name="descent",
        )
        sol, res = call(
            right_side.reshape(3, OWN_ROWS, 128),
            precond.reshape(OWN_ROWS, 128),
            viscosity.reshape(1, 1024),
            stiffness,
            element_nodes,
            live,
            shared,
            parents,
        )
        return sol.reshape(3, OWN_ROWS * 128), res.reshape(3, OWN_ROWS * 128)

    return local


def solution(mesh):
    both = ("grp", "cur")
    in_specs = (
        P(None, both),
        P(both),
        P(both),
        P(),
        P(None, both),
        P(both),
        P(None, both),
        P(None, both),
    )
    out_specs = (P(None, both), P(None, both))
    return jax.shard_map(
        make_local(mesh.shape["grp"], mesh.shape["cur"]),
        mesh=mesh,
        in_specs=in_specs,
        out_specs=out_specs,
        check_vma=False,
    )
```
